256 devices in a mesh: dp: 32 (over z, x_lo, core), tp: 8 (over y, x_hi).
Axes of the slice: x: 4 (x_hi: 2, x_lo: 2; x = x_hi * 2 + x_lo), y: 4, z: 8, core: 2. Of those that a mesh axis runs over, the one named last changes fastest.
Arguments:
- hidden: bfloat16 [1024, 4, 5120], P('dp', None, 'tp'), may hold values from -6 to 6
- norm_gain: bfloat16 [5120], P('tp'), may hold values from 0.3984375 to 2.5
- w_query: bfloat16 [5120, 4096], P(None, 'tp'), may hold values from -0.078125 to 0.078125
- key_projection: bfloat16 [5120, 1024], P(None, 'tp'), may hold values from -0.078125 to 0.078125
- value_projection: bfloat16 [5120, 1024], P(None, 'tp'), may hold values from -0.078125 to 0.078125
- query_gain: bfloat16 [128], replicated, may hold values from 0.5 to 2
- key_gain: bfloat16 [128], replicated, may hold values from 0.5 to 2
- cache_keys: bfloat16 [32, 32, 2, 128, 1024], P('dp', None, None, None, 'tp'), may hold values from -400 to 400
- cached_value_pages: bfloat16 [32, 32, 2, 128, 1024], P('dp', None, None, None, 'tp'), may hold values from -6 to 6
- cache_len: int32 [1024], replicated, may hold values from 1 to 256, as said below
- remaining: int32 [1024], P('dp'), may hold values from 0 to 7
- page_row: int32 [32, 32, 2], replicated, may hold values from 0 to 32, as said below
- page_seq: int32 [32, 32, 2], replicated, may hold values from 0 to 1, as said below
Outputs:
- attention: bfloat16 [1024, 4, 4096], P('dp', None, 'tp')
- new_keys: bfloat16 [1024, 4, 1024], P('dp', None, 'tp')
- new_values: bfloat16 [1024, 4, 1024], P('dp', None, 'tp')
The draws below stay inside these ranges and needn't reach their ends.
Inputs may be any that keep to these rules, and one draw needn't show every extreme that they name: `cache_len`: the pages of a row of n cached tokens fill exactly ceil(n / 128) slots. `page_row`: for holder group g, owner group o and slot c: the owner's row whose page the slot holds, or 32 for an empty slot. `page_seq`: each page number 0 to ceil(n / 128) - 1 of a row of n cached tokens appears once among the row's slots; empty slots hold 0.
All inputs are finite; a program needn't handle non-finite values.
Results may differ from the reference program's by a relative error of at most 0.015.
The reference program's roundings to bfloat16 on the way count: a program that leaves them out, or rounds other values in their place, can miss the bound.
Values may be sent and summed in bfloat16 or wider, within the bound.
No kernel may reach another device: no remote copies, remote signals or barrier semaphores. Data moves between devices by JAX's collectives and lax.ppermute only.
A program may use at most 64 MiB of HBM per device.

```python
import math
import jax
import jax.numpy as jnp
from jax import lax

MODEL_WIDTH = 5120
HQ = 32
KEY_VALUE_HEADS = 8
HEAD_SIZE = 128
ROWS_DEV = 32
STEPS = 4
PAGE_TOKENS = 128
GROUP_ROW_SLOTS = 2
REPLICA_GROUPS = 32
ROWS = 1024
GROUP_SLOTS = 64
MAXP = 2


def group_state(base_key):
    state_key = jax.random.fold_in(base_key, 14)
    finished_groups = jax.random.randint(state_key, (REPLICA_GROUPS,), 0, 2)
    return finished_groups.at[0].set(0).at[1].set(1)


def page_layout(base_key):
    count_key = jax.random.fold_in(base_key, 11)
    tail_key = jax.random.fold_in(base_key, 12)
    shuffle_key = jax.random.fold_in(base_key, 13)
    counts = jax.random.randint(count_key, (REPLICA_GROUPS, ROWS_DEV), 1, MAXP + 1)
    counts = counts.at[0, 0].set(MAXP).at[0, 1].set(1)
    tails = jax.random.randint(tail_key, (REPLICA_GROUPS, ROWS_DEV), 1, PAGE_TOKENS + 1)
    tails = tails.at[0, 0].set(PAGE_TOKENS)
    return (counts, tails, shuffle_key)


def page_table(base_key):
    counts, tails, shuffle_key = page_layout(base_key)
    finished_groups = group_state(base_key)
    ends = jnp.cumsum(counts, axis=1)
    starts = ends - counts
    rank_position = jnp.arange(GROUP_SLOTS, dtype=jnp.int32)
    row_of = jnp.sum((rank_position[None, :, None] >= ends[:, None, :]).astype(jnp.int32), axis=2)
    safe_row = jnp.minimum(row_of, ROWS_DEV - 1)
    seq_of = jnp.where(row_of < ROWS_DEV, rank_position[None, :] - jnp.take_along_axis(starts, safe_row, axis=1), 0)
    random_jitter = jax.random.randint(shuffle_key, (REPLICA_GROUPS, GROUP_SLOTS), 0, 2 ** 20)
    holder_reward = finished_groups[rank_position // GROUP_ROW_SLOTS] * 2 ** 21
    group_scores = (random_jitter + holder_reward[None, :]) * GROUP_SLOTS + rank_position[None, :]
    placed = jnp.argsort(-group_scores, axis=1)
    inverse = jnp.argsort(placed, axis=1)
    row_slot = jnp.take_along_axis(row_of, inverse, axis=1)
    seq_slot = jnp.take_along_axis(seq_of, inverse, axis=1)
    row_table = row_slot.reshape(REPLICA_GROUPS, REPLICA_GROUPS, GROUP_ROW_SLOTS).transpose(1, 0, 2)
    seq_table = seq_slot.reshape(REPLICA_GROUPS, REPLICA_GROUPS, GROUP_ROW_SLOTS).transpose(1, 0, 2)
    return (row_table.astype(jnp.int32), seq_table.astype(jnp.int32))


def draw_cache_len(key, part):
    counts, tails, shuffle_key = page_layout(key)
    return ((counts - 1) * PAGE_TOKENS + tails).reshape(-1).astype(jnp.int32)


def draw_page_row(key, part):
    row_table, seq_table = page_table(key)
    return row_table


def draw_page_seq(key, part):
    row_table, seq_table = page_table(key)
    return seq_table


def draw_remaining(key, part):
    finished_groups = group_state(key)
    key = jax.random.fold_in(key, 4)
    busy_left = jax.random.randint(jax.random.fold_in(key, 1), (REPLICA_GROUPS, ROWS_DEV), 2, 8)
    done_left = jax.random.randint(jax.random.fold_in(key, 2), (REPLICA_GROUPS, ROWS_DEV), 0, 2)
    left = jnp.where(finished_groups[:, None] == 1, done_left, busy_left)
    left = left.at[0, 0].set(7).at[1, 0].set(0)
    return left.reshape(-1).astype(jnp.int32)


def draw_cache_keys(key, part):
    key = jax.random.fold_in(key, 5)
    base_offset = jax.random.normal(key, (REPLICA_GROUPS, REPLICA_GROUPS, GROUP_ROW_SLOTS, PAGE_TOKENS, KEY_VALUE_HEADS * HEAD_SIZE), jnp.float32)
    return jnp.clip(base_offset, -6.0, 6.0).astype(jnp.bfloat16)


def block_scale(own_key, extent, cuts, smallest, largest):
    loudness, own = 1.0, jax.random.fold_in(own_key, 6)
    for dim, shards_of in cuts:
        steps = jnp.exp(jax.random.uniform(jax.random.fold_in(own, dim), (shards_of,), jnp.float32, smallest / len(cuts), largest / len(cuts)))
        loudness = loudness * jnp.repeat(steps, extent[dim] // shards_of).reshape([-1 if axis == dim else 1 for axis in range(len(extent))])
    return loudness


def centred(rng, shape, spread, limit, shards=(), kind=jnp.bfloat16):
    entries = jax.random.normal(rng, shape, jnp.float32) * spread
    if len(shards) > 0:
        entries = block_scale(rng, shape, shards, -0.22, 0.18) * entries
    return jnp.clip(entries, min=-limit, max=limit).astype(kind)


def setup_inputs(seed: int = 0) -> dict:
    splits = jax.random.split(jax.random.key(seed), 14)
    hidden = centred(splits[0], (ROWS, STEPS, MODEL_WIDTH), 1.0, 6.0, ((0, 32), (2, 8)))
    norm_gain = jnp.clip(jnp.exp(math.log(2.5) - 1.8364954 * jax.random.uniform(splits[1], (MODEL_WIDTH,), jnp.float32) ** block_scale(splits[1], (MODEL_WIDTH,), ((0, 8),), -0.2, 0.2)), 0.3984375, 2.5).astype(jnp.bfloat16)
    w_query = centred(splits[2], (MODEL_WIDTH, HQ * HEAD_SIZE), MODEL_WIDTH ** -0.5, 0.078125, ((1, 8),))
    key_projection = centred(splits[3], (MODEL_WIDTH, KEY_VALUE_HEADS * HEAD_SIZE), MODEL_WIDTH ** -0.5, 0.078125, ((1, 8),))
    value_projection = centred(splits[4], (MODEL_WIDTH, KEY_VALUE_HEADS * HEAD_SIZE), MODEL_WIDTH ** -0.5, 0.078125, ((1, 8),))
    query_gain = jnp.clip(jnp.exp(jax.random.uniform(splits[5], (HEAD_SIZE,), jnp.float32, math.log(0.5), math.log(2.0))), 0.5, 2.0).astype(jnp.bfloat16)
    key_gain = jnp.clip(jnp.exp(jax.random.uniform(splits[6], (HEAD_SIZE,), jnp.float32, math.log(0.5), math.log(2.0))), 0.5, 2.0).astype(jnp.bfloat16)
    cache_keys = draw_cache_keys(jax.random.fold_in(splits[13], 71), 0)
    cached_value_pages = centred(splits[8], (REPLICA_GROUPS, REPLICA_GROUPS, GROUP_ROW_SLOTS, PAGE_TOKENS, KEY_VALUE_HEADS * HEAD_SIZE), 1.0, 6.0, ((0, 32), (4, 8)))
    cache_len = draw_cache_len(jax.random.fold_in(splits[13], 71), 0)
    remaining = draw_remaining(jax.random.fold_in(splits[13], 71), 0)
    page_row = draw_page_row(jax.random.fold_in(splits[13], 71), 0)
    page_seq = draw_page_seq(jax.random.fold_in(splits[13], 71), 0)
    return {"hidden": hidden, "norm_gain": norm_gain, "w_query": w_query, "key_projection": key_projection, "value_projection": value_projection, "query_gain": query_gain, "key_gain": key_gain, "cache_keys": cache_keys, "cached_value_pages": cached_value_pages, "cache_len": cache_len, "remaining": remaining, "page_row": page_row, "page_seq": page_seq}


EPSILON = 1e-06
ROPE_BASE = 1000000.0
MASKED_SCORE = -1e+30

def head_norm_rope(heads, gain_vector, positions):
    head_width = heads.shape[-1]
    half_width = head_width // 2
    scaled = heads * lax.rsqrt(lax.optimization_barrier(jnp.mean(heads * heads, axis=-1, keepdims=True)) + EPSILON) * gain_vector.astype(jnp.float32)
    frequency = jnp.exp(jnp.arange(half_width, dtype=jnp.float32) * (-2.0 * math.log(ROPE_BASE) / head_width))
    angles = positions.astype(jnp.float32)[:, :, None, None] * frequency
    cosine = jnp.cos(angles)
    sine_part = jnp.sin(angles)
    first_half = scaled[..., :half_width]
    second = scaled[..., half_width:]
    return jnp.concatenate([first_half * cosine - second * sine_part, second * cosine + first_half * sine_part], axis=-1)

def masked_parts(group_scores, usable):
    group_scores = jnp.where(usable, group_scores, MASKED_SCORE)
    block_max = lax.optimization_barrier(jnp.max(group_scores, axis=-1))
    weights = jnp.where(usable, jnp.exp(group_scores - block_max[..., None]), 0.0).astype(jnp.bfloat16)
    return (block_max, weights, lax.optimization_barrier(jnp.sum(weights.astype(jnp.float32), axis=-1)))

def page_partial(queries, page_keys, page_values, usable):
    scale = 1.0 / math.sqrt(queries.shape[-1])
    group_scores = jnp.einsum('nkqd,npkd->nkqp', queries.astype(jnp.float32), page_keys.astype(jnp.float32)) * scale
    block_max, weights, block_total = masked_parts(group_scores, usable[:, None, None, :])
    output = jnp.einsum('nkqp,npkd->nkqd', weights.astype(jnp.float32), page_values.astype(jnp.float32))
    return (block_max, block_total, output)

def new_partial(arranged, fresh_keys, fresh_values, step_count):
    scale = 1.0 / math.sqrt(arranged.shape[-1])
    group_scores = jnp.einsum('rkqd,rjkd->rkqj', arranged.astype(jnp.float32), fresh_keys.astype(jnp.float32)) * scale
    step_index = jnp.arange(arranged.shape[2], dtype=jnp.int32) % step_count
    causal = jnp.arange(step_count, dtype=jnp.int32)[None, :] <= step_index[:, None]
    block_max, weights, block_total = masked_parts(group_scores, causal[None, None])
    output = jnp.einsum('rkqj,rjkd->rkqd', weights.astype(jnp.float32), fresh_values.astype(jnp.float32))
    return (block_max, block_total, output)

def combine_pages(page_rows, page_max, page_total, page_out, new_max, new_total, new_out, row_count):
    row_hit = (page_rows[:, None] == jnp.arange(row_count, dtype=jnp.int32)[None, :])[:, :, None, None]
    page_top = lax.optimization_barrier(jnp.max(jnp.where(row_hit, page_max[:, None], MASKED_SCORE), axis=0))
    row_max = jnp.maximum(page_top, new_max)
    factor = jnp.exp(jnp.where(row_hit, page_max[:, None] - row_max[None], MASKED_SCORE))
    own_factor = jnp.exp(new_max - row_max)
    denominator = jnp.einsum('nrkq,nkq->rkq', factor, page_total, precision=lax.Precision.HIGHEST) + own_factor * new_total
    numerator = jnp.einsum('nrkq,nkqd->rkqd', factor, page_out, precision=lax.Precision.HIGHEST) + own_factor[..., None] * new_out
    return numerator / denominator[..., None]

def reference(hidden, norm_gain, w_query, key_projection, value_projection, query_gain, key_gain, cache_keys, cached_value_pages, cache_len, remaining, page_row, page_seq):
    row_count, step_count, feature_count = hidden.shape
    head_width = query_gain.shape[0]
    groups = page_row.shape[0]
    per_group = row_count // groups
    page_len = cache_keys.shape[3]
    hidden_wide = hidden.astype(jnp.float32)
    normed = (hidden_wide * lax.rsqrt(lax.optimization_barrier(jnp.mean(hidden_wide * hidden_wide, axis=-1, keepdims=True)) + EPSILON) * norm_gain.astype(jnp.float32)).astype(jnp.bfloat16)
    flattened = normed.reshape(row_count * step_count, feature_count)
    positions = cache_len[:, None] + jnp.arange(step_count, dtype=jnp.int32)[None, :]
    queries = jnp.dot(flattened, w_query, preferred_element_type=jnp.float32).reshape(row_count, step_count, -1, head_width)
    queries = head_norm_rope(queries, query_gain, positions).astype(jnp.bfloat16)
    fresh_keys = jnp.dot(flattened, key_projection, preferred_element_type=jnp.float32).reshape(row_count, step_count, -1, head_width)
    fresh_keys = head_norm_rope(fresh_keys, key_gain, positions).astype(jnp.bfloat16)
    fresh_values = jnp.dot(flattened, value_projection, preferred_element_type=jnp.float32).astype(jnp.bfloat16).reshape(row_count, step_count, -1, head_width)
    kv_heads = fresh_keys.shape[2]
    group_size = queries.shape[2] // kv_heads
    arranged = queries.reshape(row_count, step_count, kv_heads, group_size, head_width).transpose(0, 2, 3, 1, 4).reshape(row_count, kv_heads, group_size * step_count, head_width)
    new_max, new_total, new_out = new_partial(arranged, fresh_keys, fresh_values, step_count)

    def one_owner(owner_group):
        row_start = owner_group * per_group
        owner_queries = lax.dynamic_slice_in_dim(arranged, row_start, per_group, 0)
        owner_lengths = lax.dynamic_slice_in_dim(cache_len, row_start, per_group, 0)
        page_keys = lax.dynamic_index_in_dim(cache_keys, owner_group, 1, keepdims=False).reshape(-1, page_len, kv_heads, head_width)
        page_values = lax.dynamic_index_in_dim(cached_value_pages, owner_group, 1, keepdims=False).reshape(-1, page_len, kv_heads, head_width)
        page_rows = lax.dynamic_index_in_dim(page_row, owner_group, 1, keepdims=False).reshape(-1)
        page_numbers = lax.dynamic_index_in_dim(page_seq, owner_group, 1, keepdims=False).reshape(-1)
        safe_row = jnp.minimum(page_rows, per_group - 1)
        length_cap = jnp.where(page_rows < per_group, owner_lengths[safe_row], 0)
        usable = page_numbers[:, None] * page_len + jnp.arange(page_len, dtype=jnp.int32)[None, :] < length_cap[:, None]
        page_max, page_total, page_out = page_partial(owner_queries[safe_row], page_keys, page_values, usable)
        return combine_pages(page_rows, page_max, page_total, page_out, lax.dynamic_slice_in_dim(new_max, row_start, per_group, 0), lax.dynamic_slice_in_dim(new_total, row_start, per_group, 0), lax.dynamic_slice_in_dim(new_out, row_start, per_group, 0), per_group)
    attended = lax.map(one_owner, jnp.arange(groups, dtype=jnp.int32)).reshape(row_count, kv_heads, group_size, step_count, head_width)
    attended = attended.transpose(0, 3, 1, 2, 4).reshape(row_count, step_count, -1)
    live = jnp.arange(step_count, dtype=jnp.int32)[None, :] < remaining[:, None]
    attention = jnp.where(live[:, :, None], attended, 0.0).astype(jnp.bfloat16)
    return (attention, fresh_keys.reshape(row_count, step_count, -1), fresh_values.reshape(row_count, step_count, -1))
```

```python
import functools
import math

import jax
import jax.numpy as jnp
from jax import lax
from jax.experimental import pallas as pl
from jax.experimental.pallas import tpu as pltpu
from jax.sharding import PartitionSpec as P

EPSILON = 1e-06
ROPE_BASE = 1000000.0
MASKED = -1e30
ROWS = 32
STEPS = 4
HEADS = 4
QUERIES = HEADS * STEPS
WIDTH = 128
GROUPS = 32
SLOTS = 2
TOKENS = ROWS * STEPS
SIDE = 8
SCALE = 1.0 / math.sqrt(WIDTH)

VMEM = pltpu.VMEM
SMEM = pltpu.SMEM


def project_kernel(
    x_ref, wq_ref, wk_ref, wv_ref, qg_ref, kg_ref, cos_ref, sin_ref, row_ref, me_ref,
    send_ref, pack_ref, key_ref, value_ref, norm_ref,
):
    shards, _, features = x_ref.shape
    total = jnp.zeros((TOKENS, 1), jnp.float32)
    for t in range(shards):
        x = x_ref[t, :TOKENS, :].astype(jnp.float32)
        total = total + jnp.sum(x * x, axis=1, keepdims=True)
    rstd = lax.rsqrt(total * (1.0 / (shards * features)) + EPSILON)
    for t in range(shards):
        x = x_ref[t, :TOKENS, :].astype(jnp.float32)
        gain = x_ref[t, TOKENS : TOKENS + 8, :].astype(jnp.float32)[0:1]
        norm_ref[:, t * features : (t + 1) * features] = (x * rstd * gain).astype(jnp.bfloat16)
    cos = cos_ref[...]
    sin = sin_ref[...]

    def rotated(heads, gain):
        mean = jnp.sum(heads * heads, axis=1, keepdims=True) * (1.0 / WIDTH)
        scaled = heads * lax.rsqrt(mean + EPSILON) * gain
        return scaled * cos + pltpu.roll(scaled, WIDTH // 2, 1) * sin

    normed = norm_ref[...]
    queries = jnp.dot(normed, wq_ref[...], preferred_element_type=jnp.float32)
    q_gain = qg_ref[...].astype(jnp.float32)
    low = lax.broadcasted_iota(jnp.int32, (8, WIDTH), 0) < STEPS
    turned = [
        rotated(queries[:, h * WIDTH : (h + 1) * WIDTH], q_gain) for h in range(HEADS)
    ]
    for i in range(ROWS // 2):
        parts = [turned[h][8 * i : 8 * i + 8] for h in range(HEADS)]
        rolled = [pltpu.roll(p, STEPS, 0) for p in parts]
        even = [jnp.where(low, parts[h], rolled[h + 1]) for h in (0, 2)]
        odd = [jnp.where(low, rolled[h], parts[h + 1]) for h in (0, 2)]
        pack_ref[2 * i] = jnp.concatenate(even, axis=0).astype(jnp.bfloat16)
        pack_ref[2 * i + 1] = jnp.concatenate(odd, axis=0).astype(jnp.bfloat16)
    me = me_ref[0]
    for g in range(GROUPS):
        for c in range(SLOTS):
            row = jnp.minimum(row_ref[(g * GROUPS + me) * SLOTS + c], ROWS - 1)
            send_ref[g, c * QUERIES : (c + 1) * QUERIES, :] = pack_ref[row]
    keys = jnp.dot(normed, wk_ref[...], preferred_element_type=jnp.float32)
    key_ref[...] = rotated(keys, kg_ref[...].astype(jnp.float32)).astype(jnp.bfloat16)
    values = jnp.dot(normed, wv_ref[...], preferred_element_type=jnp.float32)
    value_ref[...] = values.astype(jnp.bfloat16)


def fresh_kernel(pack_ref, key_ref, value_ref, lse_ref, out_ref):
    count = ROWS * QUERIES
    scores = (
        lax.dot_general(
            pack_ref[...].reshape(count, WIDTH), key_ref[...],
            (((1,), (1,)), ((), ())), preferred_element_type=jnp.float32,
        )
        * SCALE
    )
    query = lax.broadcasted_iota(jnp.int32, (count, TOKENS), 0)
    token = lax.broadcasted_iota(jnp.int32, (count, TOKENS), 1)
    usable = ((query >> 4) == (token >> 2)) & ((token & 3) <= (query & 3))
    scores = jnp.where(usable, scores, MASKED)
    top = jnp.max(scores, axis=1, keepdims=True)
    weights = jnp.where(usable, jnp.exp(scores - top), 0.0).astype(jnp.bfloat16)
    total = jnp.sum(weights.astype(jnp.float32), axis=1, keepdims=True)
    out = jnp.dot(weights, value_ref[...], preferred_element_type=jnp.float32)
    out_ref[...] = out / total
    lse_ref[...] = jnp.broadcast_to(top + jnp.log(total), (count, WIDTH))


def page_kernel(q_ref, key_ref, value_ref, len_ref, row_ref, seq_ref, me_ref, send_ref):
    me = me_ref[0]
    lane = lax.broadcasted_iota(jnp.int32, (QUERIES, WIDTH), 1)
    wide_lane = lax.broadcasted_iota(jnp.int32, (SLOTS * QUERIES, WIDTH), 1)
    side = jnp.zeros((SLOTS * QUERIES, WIDTH), jnp.float32)
    for o in range(GROUPS):
        column = []
        for c in range(SLOTS):
            slot = o * SLOTS + c
            place = (me * GROUPS + o) * SLOTS + c
            row = row_ref[place]
            length = len_ref[o * ROWS + jnp.minimum(row, ROWS - 1)]
            cap = jnp.where(row < ROWS, length - seq_ref[place] * WIDTH, 0)
            usable = lane < cap
            scores = (
                lax.dot_general(
                    q_ref[o, c * QUERIES : (c + 1) * QUERIES, :], key_ref[slot],
                    (((1,), (1,)), ((), ())), preferred_element_type=jnp.float32,
                )
                * SCALE
            )
            scores = jnp.where(usable, scores, MASKED)
            top = jnp.max(scores, axis=1, keepdims=True)
            weights = jnp.where(usable, jnp.exp(scores - top), 0.0).astype(jnp.bfloat16)
            total = jnp.sum(weights.astype(jnp.float32), axis=1, keepdims=True)
            out = jnp.dot(weights, value_ref[slot], preferred_element_type=jnp.float32)
            safe = jnp.maximum(total, 1e-30)
            send_ref[o, c * QUERIES : (c + 1) * QUERIES, :] = (out / safe).astype(jnp.bfloat16)
            column.append(top + jnp.log(safe))
        side = jnp.where(wide_lane == o, jnp.concatenate(column, axis=0), side)
    pairs = SLOTS * QUERIES
    square = jnp.concatenate([side, jnp.zeros((WIDTH - pairs, WIDTH), jnp.float32)], axis=0).T
    whole = square[:GROUPS]
    high = whole.astype(jnp.bfloat16).astype(jnp.float32)
    rest = whole - high
    middle = rest.astype(jnp.bfloat16).astype(jnp.float32)
    last = rest - middle
    pieces = high + pltpu.roll(middle, pairs, 1) + pltpu.roll(last, 2 * pairs, 1)
    for o in range(GROUPS):
        send_ref[o, pairs : pairs + SIDE, :] = jnp.broadcast_to(
            pieces[o : o + 1], (SIDE, WIDTH)
        ).astype(jnp.bfloat16)


def combine_kernel(
    got_ref, lse_ref, out_ref, row_ref, seq_ref, me_ref, remaining_ref,
    attention_ref, wide_ref, index_ref,
):
    me = me_ref[0]
    pairs = SLOTS * QUERIES
    none = GROUPS * SLOTS
    for i in range(ROWS * SLOTS):
        index_ref[i] = none
    for g in range(GROUPS):
        for c in range(SLOTS):
            place = (g * GROUPS + me) * SLOTS + c
            row = row_ref[place]
            index_ref[jnp.where(row < ROWS, row * SLOTS + seq_ref[place], none)] = g * SLOTS + c
    sub = lax.broadcasted_iota(jnp.int32, (8, WIDTH), 0)
    blocks = []
    for b in range(GROUPS // 8):
        block = jnp.zeros((8, WIDTH), jnp.float32)
        for i in range(8):
            tile = got_ref[8 * b + i, pairs : pairs + SIDE, :].astype(jnp.float32)
            block = jnp.where(sub == i, tile, block)
        blocks.append(block)
    side = jnp.concatenate(blocks, axis=0)
    side = side + pltpu.roll(side, WIDTH - pairs, 1) + pltpu.roll(side, WIDTH - 2 * pairs, 1)
    square = jnp.concatenate([side, jnp.zeros((WIDTH - GROUPS, WIDTH), jnp.float32)], axis=0).T
    for g in range(GROUPS):
        for c in range(SLOTS):
            wide_ref[g * SLOTS + c] = jnp.broadcast_to(
                square[c * QUERIES : (c + 1) * QUERIES, g : g + 1], (QUERIES, WIDTH)
            )
    wide_ref[none] = jnp.full((QUERIES, WIDTH), MASKED, jnp.float32)
    step = lax.broadcasted_iota(jnp.int32, (QUERIES, WIDTH), 0) & (STEPS - 1)
    for r in range(ROWS):
        lses = [lse_ref[r * QUERIES : (r + 1) * QUERIES, :]]
        outs = [out_ref[r * QUERIES : (r + 1) * QUERIES, :]]
        for k in range(SLOTS):
            slot = index_ref[r * SLOTS + k]
            lses.append(wide_ref[slot])
            known = jnp.minimum(slot, none - 1)
            start = pl.multiple_of((known & (SLOTS - 1)) * QUERIES, QUERIES)
            outs.append(got_ref[known >> 1, pl.ds(start, QUERIES), :].astype(jnp.float32))
        top = functools.reduce(jnp.maximum, lses)
        factors = [jnp.exp(l - top) for l in lses]
        above = sum(f * o for f, o in zip(factors, outs))
        result = above / sum(factors)
        result = jnp.where(step < remaining_ref[r], result, 0.0).astype(jnp.bfloat16)
        for h in range(HEADS):
            attention_ref[r, :, h * WIDTH : (h + 1) * WIDTH] = result[
                h * STEPS : (h + 1) * STEPS, :
            ]


def shards(
    hidden, norm_gain, w_query, key_projection, value_projection, query_gain, key_gain,
    cache_keys, cached_value_pages, cache_len, remaining, page_row, page_seq,
):
    features = hidden.shape[2]
    tensor = lax.axis_size("tp")
    me = lax.axis_index("dp")
    block = jnp.concatenate(
        [
            hidden.reshape(TOKENS, features),
            jnp.broadcast_to(norm_gain[None, :], (8, features)),
        ],
        axis=0,
    )
    gathered = lax.all_to_all(
        jnp.broadcast_to(block[None], (tensor,) + block.shape), "tp",
        split_axis=0, concat_axis=0, tiled=True,
    )
    lengths = lax.dynamic_slice_in_dim(cache_len, me * ROWS, ROWS)
    positions = (lengths[:, None] + jnp.arange(STEPS, dtype=jnp.int32)[None, :]).reshape(-1, 1)
    frequency = jnp.exp(
        jnp.arange(WIDTH // 2, dtype=jnp.float32) * (-2.0 * math.log(ROPE_BASE) / WIDTH)
    )
    angles = positions.astype(jnp.float32) * frequency[None, :]
    cos = jnp.cos(angles)
    sin = jnp.sin(angles)
    cos = jnp.concatenate([cos, cos], axis=1)
    sin = jnp.concatenate([-sin, sin], axis=1)
    mine = me.reshape(1).astype(jnp.int32)
    rows_flat = page_row.reshape(-1)
    seqs_flat = page_seq.reshape(-1)
    params = pltpu.CompilerParams(vmem_limit_bytes=48 * 1024 * 1024)

    def vmem(n):
        return [pl.BlockSpec(memory_space=VMEM)] * n

    def smem(n):
        return [pl.BlockSpec(memory_space=SMEM)] * n

    send_q, pack, new_key, new_value = pl.pallas_call(
        project_kernel,
        out_shape=(
            jax.ShapeDtypeStruct((GROUPS, SLOTS * QUERIES, WIDTH), jnp.bfloat16),
            jax.ShapeDtypeStruct((ROWS, QUERIES, WIDTH), jnp.bfloat16),
            jax.ShapeDtypeStruct((TOKENS, WIDTH), jnp.bfloat16),
            jax.ShapeDtypeStruct((TOKENS, WIDTH), jnp.bfloat16),
        ),
        in_specs=vmem(8) + smem(2),
        out_specs=tuple(vmem(4)),
        scratch_shapes=[pltpu.VMEM((TOKENS, tensor * features), jnp.bfloat16)],
        compiler_params=params,
        name="project",
    )(
        gathered, w_query, key_projection, value_projection, query_gain[None, :],
        key_gain[None, :], cos, sin, rows_flat, mine,
    )
    got_q = lax.all_to_all(send_q, "dp", split_axis=0, concat_axis=0, tiled=True)
    new_lse, new_out = pl.pallas_call(
        fresh_kernel,
        out_shape=(
            jax.ShapeDtypeStruct((ROWS * QUERIES, WIDTH), jnp.float32),
            jax.ShapeDtypeStruct((ROWS * QUERIES, WIDTH), jnp.float32),
        ),
        in_specs=vmem(3),
        out_specs=tuple(vmem(2)),
        compiler_params=params,
        name="fresh",
    )(pack, new_key, new_value)
    send_out = pl.pallas_call(
        page_kernel,
        out_shape=jax.ShapeDtypeStruct((GROUPS, SLOTS * QUERIES + SIDE, WIDTH), jnp.bfloat16),
        in_specs=vmem(3) + smem(4),
        out_specs=vmem(1)[0],
        compiler_params=params,
        name="pages",
    )(
        got_q,
        cache_keys.reshape(GROUPS * SLOTS, WIDTH, WIDTH),
        cached_value_pages.reshape(GROUPS * SLOTS, WIDTH, WIDTH),
        cache_len, rows_flat, seqs_flat, mine,
    )
    got_out = lax.all_to_all(send_out, "dp", split_axis=0, concat_axis=0, tiled=True)
    attention = pl.pallas_call(
        combine_kernel,
        out_shape=jax.ShapeDtypeStruct((ROWS, STEPS, HEADS * WIDTH), jnp.bfloat16),
        in_specs=vmem(3) + smem(4),
        out_specs=vmem(1)[0],
        scratch_shapes=[
            pltpu.VMEM((GROUPS * SLOTS + 1, QUERIES, WIDTH), jnp.float32),
            pltpu.SMEM((ROWS * SLOTS + 8,), jnp.int32),
        ],
        compiler_params=params,
        name="combine",
    )(got_out, new_lse, new_out, rows_flat, seqs_flat, mine, remaining)
    return (
        attention,
        new_key.reshape(ROWS, STEPS, WIDTH),
        new_value.reshape(ROWS, STEPS, WIDTH),
    )


def solution(mesh):
    in_specs = (
        P("dp", None, "tp"),
        P("tp"),
        P(None, "tp"),
        P(None, "tp"),
        P(None, "tp"),
        P(),
        P(),
        P("dp", None, None, None, "tp"),
        P("dp", None, None, None, "tp"),
        P(),
        P("dp"),
        P(),
        P(),
    )
    out_specs = (P("dp", None, "tp"), P("dp", None, "tp"), P("dp", None, "tp"))
    return jax.shard_map(shards, mesh=mesh, in_specs=in_specs, out_specs=out_specs, check_vma=False)
```

```python
import functools
import math

import jax
import jax.numpy as jnp
from jax import lax
from jax.experimental import pallas as pl
from jax.experimental.pallas import tpu as pltpu
from jax.sharding import PartitionSpec as P

EPSILON = 1e-06
ROPE_BASE = 1000000.0
MASKED = -1e30
ROWS = 32
STEPS = 4
HEADS = 4
QUERIES = HEADS * STEPS
WIDTH = 128
GROUPS = 32
CORES = 2
CHIPS = GROUPS // CORES
SLOTS = 2
SHARED = CORES * SLOTS
TOKENS = ROWS * STEPS
SIDE = 8
SCALE = 1.0 / math.sqrt(WIDTH)

VMEM = pltpu.VMEM
SMEM = pltpu.SMEM


def slot_row(row_ref, holder, owner, c):
    return row_ref[(holder * GROUPS + owner) * SLOTS + c]


def spread_kernel(hidden_hbm, gain_hbm, out_ref, hidden_ref, gain_ref, block_ref, sem):
    features = hidden_hbm.shape[2]
    copies = [
        pltpu.make_async_copy(hidden_hbm, hidden_ref, sem.at[0]),
        pltpu.make_async_copy(gain_hbm, gain_ref, sem.at[1]),
    ]
    for copy in copies:
        copy.start()
    for copy in copies:
        copy.wait()
    tiles = features // WIDTH
    for i in range(0, ROWS, 4):
        part = [hidden_ref[i + k].astype(jnp.float32) for k in range(4)]
        part = jnp.concatenate(part, axis=0).astype(jnp.bfloat16)
        for f in range(tiles):
            first = f * TOKENS + i * STEPS
            block_ref[first : first + 4 * STEPS, :] = part[:, f * WIDTH : (f + 1) * WIDTH]
    gain = gain_ref[...].astype(jnp.float32)
    gain = jnp.concatenate([gain, jnp.zeros((16 - tiles, WIDTH), jnp.float32)], axis=0)
    block_ref[tiles * TOKENS : tiles * TOKENS + 16, :] = gain.astype(jnp.bfloat16)
    copies = [
        pltpu.make_async_copy(block_ref, out_ref.at[t], sem.at[2 + t])
        for t in range(out_ref.shape[0])
    ]
    for copy in copies:
        copy.start()
    for copy in copies:
        copy.wait()


def table_kernel(
    cos_ref, sin_ref, qg_ref, kg_ref, key_hbm, value_hbm, len_ref, row_ref, seq_ref, me_ref,
    turn_out, cap_out, keep_hbm, give_hbm, sem,
):
    me = me_ref[0]
    core = lax.rem(me, CORES)
    copies = []
    for n, pages in enumerate((key_hbm, value_hbm)):
        copies.append(pltpu.make_async_copy(pages.at[:, core], keep_hbm.at[n], sem.at[2 * n]))
        copies.append(
            pltpu.make_async_copy(pages.at[:, 1 - core], give_hbm.at[n], sem.at[2 * n + 1])
        )
    for copy in copies:
        copy.start()
    cos = cos_ref[...]
    sin = sin_ref[...]
    cos = jnp.concatenate([cos, cos], axis=1)
    sin = jnp.concatenate([-sin, sin], axis=1)
    for n, gain_ref in enumerate((qg_ref, kg_ref)):
        gain = jnp.broadcast_to(gain_ref[...].astype(jnp.float32), (8, WIDTH))
        other = pltpu.roll(gain, WIDTH // 2, 1)
        turn_out[2 * n] = cos * gain[0:1]
        turn_out[2 * n + 1] = sin * other[0:1]
    lane = lax.broadcasted_iota(jnp.int32, (1, WIDTH), 1) // QUERIES
    for j in range(GROUPS * SLOTS // 8):
        cap = jnp.zeros((1, WIDTH), jnp.int32)
        for i in range(8):
            chip, k, c = 2 * j + i // SHARED, i // SLOTS % CORES, i % SLOTS
            owner = chip * CORES + core
            holder = me if k == 0 else me + 1 - 2 * core
            place = (holder * GROUPS + owner) * SLOTS + c
            row = row_ref[place]
            length = len_ref[owner * ROWS + jnp.minimum(row, ROWS - 1)]
            cap = jnp.where(
                lane == i, jnp.where(row < ROWS, length - seq_ref[place] * WIDTH, 0), cap
            )
        cap_out[j : j + 1, :] = cap
    for copy in copies:
        copy.wait()


def rotated(heads, cos, sin):
    mean = jnp.sum(heads * heads, axis=1, keepdims=True) * (1.0 / WIDTH)
    scaled = heads * lax.rsqrt(mean + EPSILON)
    return scaled * cos + pltpu.roll(scaled, WIDTH // 2, 1) * sin


def project_kernel(
    x_ref, wq_ref, turn_ref, me_ref, row_hbm,
    send_ref, pack_ref, norm_hbm, norm_ref, row_ref, sem,
):
    rows_copy = pltpu.make_async_copy(row_hbm, row_ref, sem.at[0])
    rows_copy.start()
    count = x_ref.shape[0]
    tiles = wq_ref.shape[0] // count // WIDTH

    def block(n):
        t, f = n // tiles, n % tiles
        return x_ref[t, f * TOKENS : (f + 1) * TOKENS, :].astype(jnp.float32)

    total = jnp.zeros((TOKENS, WIDTH), jnp.float32)
    for n in range(count * tiles):
        x = block(n)
        total = total + x * x
    total = jnp.sum(total, axis=1, keepdims=True)
    rstd = lax.rsqrt(total * (1.0 / (count * tiles * WIDTH)) + EPSILON)
    queries = jnp.zeros((TOKENS, HEADS * WIDTH), jnp.float32)
    chunk = 2 * tiles
    copies = []
    for s in range(0, count * tiles, chunk):
        parts = []
        for n in range(s, s + chunk):
            t, f = n // tiles, n % tiles
            last = tiles * TOKENS
            gain = x_ref[t, last : last + 16, :].astype(jnp.float32)[f : f + 1]
            parts.append((block(n) * rstd * gain).astype(jnp.bfloat16))
        part = jnp.concatenate(parts, axis=1)
        span = slice(s * WIDTH, (s + chunk) * WIDTH)
        norm_ref[:, span] = part
        copies.append(
            pltpu.make_async_copy(
                norm_ref.at[:, span], norm_hbm.at[:, span], sem.at[2 + s // chunk]
            )
        )
        copies[-1].start()
        queries += jnp.dot(part, wq_ref[span, :], preferred_element_type=jnp.float32)
    low = lax.broadcasted_iota(jnp.int32, (8, WIDTH), 0) < STEPS
    turned = [
        rotated(queries[:, h * WIDTH : (h + 1) * WIDTH], turn_ref[0], turn_ref[1])
        for h in range(HEADS)
    ]
    for i in range(ROWS // 2):
        parts = [turned[h][8 * i : 8 * i + 8] for h in range(HEADS)]
        rolled = [pltpu.roll(p, STEPS, 0) for p in parts]
        even = [jnp.where(low, parts[h], rolled[h + 1]) for h in (0, 2)]
        odd = [jnp.where(low, rolled[h], parts[h + 1]) for h in (0, 2)]
        pack_ref[2 * i] = jnp.concatenate(even, axis=0).astype(jnp.bfloat16)
        pack_ref[2 * i + 1] = jnp.concatenate(odd, axis=0).astype(jnp.bfloat16)
    me = me_ref[0]
    rows_copy.wait()
    core = lax.rem(me, CORES)
    for chip in range(CHIPS):
        for k in range(CORES):
            holder = chip * CORES + (core if k == 0 else 1 - core)
            for c in range(SLOTS):
                row = jnp.minimum(slot_row(row_ref, holder, me, c), ROWS - 1)
                first = (k * SLOTS + c) * QUERIES
                send_ref[chip, first : first + QUERIES, :] = pack_ref[row]
    for copy in copies:
        copy.wait()


def fresh_kernel(
    norm_ref, wk_ref, wv_ref, turn_ref, pack_ref, key_ref, value_ref, max_ref, total_ref, out_ref
):
    count = ROWS * QUERIES
    normed = norm_ref[...]
    keys = jnp.dot(normed, wk_ref[...], preferred_element_type=jnp.float32)
    keys = rotated(keys, turn_ref[2], turn_ref[3]).astype(jnp.bfloat16)
    values = jnp.dot(normed, wv_ref[...], preferred_element_type=jnp.float32)
    values = values.astype(jnp.bfloat16)
    key_ref[...] = keys
    value_ref[...] = values
    scores = (
        lax.dot_general(
            pack_ref[...].reshape(count, WIDTH), keys,
            (((1,), (1,)), ((), ())), preferred_element_type=jnp.float32,
        )
        * SCALE
    )
    query = lax.broadcasted_iota(jnp.int32, (count, TOKENS), 0)
    token = lax.broadcasted_iota(jnp.int32, (count, TOKENS), 1)
    usable = ((query >> 4) == (token >> 2)) & ((token & 3) <= (query & 3))
    scores = jnp.where(usable, scores, MASKED)
    top = jnp.max(scores, axis=1, keepdims=True)
    weights = jnp.where(usable, jnp.exp(scores - top), 0.0).astype(jnp.bfloat16)
    total = jnp.sum(weights.astype(jnp.float32), axis=1, keepdims=True)
    out_ref[...] = jnp.dot(weights, values, preferred_element_type=jnp.float32)
    max_ref[...] = jnp.broadcast_to(top, (count, WIDTH))
    total_ref[...] = jnp.broadcast_to(total, (count, WIDTH))


def in_pieces(x):
    high = x.astype(jnp.bfloat16).astype(jnp.float32)
    rest = x - high
    middle = rest.astype(jnp.bfloat16).astype(jnp.float32)
    return [high, middle, rest - middle]


def page_kernel(
    q_ref, keep_ref, got_ref, cap_ref, send_hbm, send_ref, score_ref, weight_ref, sem
):
    token = lax.broadcasted_iota(jnp.int32, (WIDTH, WIDTH), 0)
    member = lax.broadcasted_iota(jnp.int32, (WIDTH, WIDTH), 1) // QUERIES
    side_row = lax.broadcasted_iota(jnp.int32, (SIDE, WIDTH), 0)
    batches = GROUPS * SLOTS // 8
    pairs = SHARED * QUERIES

    def page(n, slot):
        chip, k, c = slot // SHARED, slot // SLOTS % CORES, slot % SLOTS
        return (keep_ref if k == 0 else got_ref)[n, chip, c]

    zero = jnp.zeros((), jnp.bfloat16)
    for j in range(batches):
        queries = q_ref[2 * j : 2 * j + 2].reshape(WIDTH, WIDTH)
        turned = queries.astype(jnp.float32).T.astype(jnp.bfloat16)
        keys = jnp.concatenate([page(0, 8 * j + i) for i in range(8)], axis=1)
        spread = jnp.concatenate([jnp.where(member == i, turned, zero) for i in range(8)], axis=0)
        scores = jnp.dot(keys, spread, preferred_element_type=jnp.float32) * SCALE
        score_ref[j * WIDTH : (j + 1) * WIDTH, :] = jnp.where(
            token < cap_ref[j : j + 1, :], scores, MASKED
        )
    for j in range(batches):
        scores = score_ref[j * WIDTH : (j + 1) * WIDTH, :]
        top = jnp.max(scores, axis=0, keepdims=True)
        weights = jnp.exp(scores - top).astype(jnp.bfloat16).astype(jnp.float32)
        total = jnp.sum(weights, axis=0, keepdims=True)
        weight_ref[j * WIDTH : (j + 1) * WIDTH, :] = weights.T.astype(jnp.bfloat16)
        tile = jnp.zeros((SIDE, WIDTH), jnp.float32)
        for n, piece in enumerate(in_pieces(top) + in_pieces(total)):
            tile = jnp.where(side_row == n, piece, tile)
        for k in range(2):
            send_ref[2 * j + k, pairs : pairs + SIDE, :] = tile.astype(jnp.bfloat16)
    for slot in range(GROUPS * SLOTS):
        out = jnp.dot(
            weight_ref[slot * QUERIES : (slot + 1) * QUERIES, :], page(1, slot),
            preferred_element_type=jnp.float32,
        )
        c = slot % SHARED
        send_ref[slot // SHARED, c * QUERIES : (c + 1) * QUERIES, :] = out.astype(jnp.bfloat16)
    send = pltpu.make_async_copy(send_ref, send_hbm, sem.at[0])
    send.start()
    send.wait()


def combine_kernel(
    got_ref, max_ref, total_ref, out_ref, me_ref, row_hbm, seq_hbm, remaining_hbm,
    attention_ref, top_wide, total_wide, index_ref, row_ref, seq_ref, remaining_ref, sem,
):
    copies = [
        pltpu.make_async_copy(row_hbm, row_ref, sem.at[0]),
        pltpu.make_async_copy(seq_hbm, seq_ref, sem.at[1]),
        pltpu.make_async_copy(remaining_hbm, remaining_ref, sem.at[2]),
    ]
    for copy in copies:
        copy.start()
    me = me_ref[0]
    core = lax.rem(me, CORES)
    pairs = SHARED * QUERIES
    none = GROUPS * SLOTS
    for i in range(ROWS * SLOTS):
        index_ref[i] = none
    sub = lax.broadcasted_iota(jnp.int32, (8, WIDTH), 0)
    tops, totals = [], []
    for b in range(CHIPS // 8):
        top_block = jnp.zeros((8, WIDTH), jnp.float32)
        total_block = jnp.zeros((8, WIDTH), jnp.float32)
        for i in range(8):
            tile = got_ref[8 * b + i, pairs : pairs + SIDE, :].astype(jnp.float32)
            top_block = jnp.where(sub == i, tile[0:1] + tile[1:2] + tile[2:3], top_block)
            total_block = jnp.where(sub == i, tile[3:4] + tile[4:5] + tile[5:6], total_block)
        tops.append(top_block)
        totals.append(total_block)
    side = jnp.concatenate(
        tops + totals + [jnp.zeros((WIDTH - 2 * CHIPS, WIDTH), jnp.float32)], axis=0
    )
    side = pltpu.roll(side, lax.rem((2 - lax.rem(me // CORES, 2)) * pairs, WIDTH), 1).T
    for chip in range(CHIPS):
        for c in range(SHARED):
            span = slice(c * QUERIES, (c + 1) * QUERIES)
            slot = chip * SHARED + c
            top_wide[slot] = jnp.broadcast_to(side[span, chip : chip + 1], (QUERIES, WIDTH))
            total_wide[slot] = jnp.broadcast_to(
                side[span, CHIPS + chip : CHIPS + chip + 1], (QUERIES, WIDTH)
            )
    top_wide[none] = jnp.full((QUERIES, WIDTH), MASKED, jnp.float32)
    total_wide[none] = jnp.zeros((QUERIES, WIDTH), jnp.float32)
    for copy in copies:
        copy.wait()
    for chip in range(CHIPS):
        for c in range(SHARED):
            holder = chip * CORES + (core if c < SLOTS else 1 - core)
            place = (holder * GROUPS + me) * SLOTS + c % SLOTS
            row = row_ref[place]
            index_ref[jnp.where(row < ROWS, row * SLOTS + seq_ref[place], none)] = (
                chip * SHARED + c
            )
    step = lax.broadcasted_iota(jnp.int32, (QUERIES, WIDTH), 0) & (STEPS - 1)
    for r in range(ROWS):
        span = slice(r * QUERIES, (r + 1) * QUERIES)
        tops, totals, outs = [max_ref[span, :]], [total_ref[span, :]], [out_ref[span, :]]
        for k in range(SLOTS):
            slot = index_ref[r * SLOTS + k]
            tops.append(top_wide[slot])
            totals.append(total_wide[slot])
            known = jnp.minimum(slot, none - 1)
            start = pl.multiple_of((known & (SHARED - 1)) * QUERIES, QUERIES)
            outs.append(got_ref[known >> 2, pl.ds(start, QUERIES), :].astype(jnp.float32))
        top = functools.reduce(jnp.maximum, tops)
        factors = [jnp.exp(t - top) for t in tops]
        above = sum(f * o for f, o in zip(factors, outs))
        below = sum(f * t for f, t in zip(factors, totals))
        result = jnp.where(step < remaining_ref[r], above / below, 0.0).astype(jnp.bfloat16)
        for h in range(HEADS):
            attention_ref[r, :, h * WIDTH : (h + 1) * WIDTH] = result[
                h * STEPS : (h + 1) * STEPS, :
            ]


SPREAD_MIB = 60
TABLE_MIB = 4
PROJECT_MIB = 8
FRESH_MIB = 8
PAGES_MIB = 6
COMBINE_MIB = 6
TABLE_COST = 20
PROJECT_COST = 10
FRESH_COST = 10


def limit(mib):
    return pltpu.CompilerParams(vmem_limit_bytes=mib * 1024 * 1024)


def cost(us):
    return pl.CostEstimate(flops=us << 30, bytes_accessed=1 << 20, transcendentals=0)


def shards(
    hidden, norm_gain, w_query, key_projection, value_projection, query_gain, key_gain,
    cache_keys, cached_value_pages, cache_len, remaining, page_row, page_seq,
):
    features = hidden.shape[2]
    tensor = lax.axis_size("tp")
    me = lax.axis_index("dp")
    mine = me.reshape(1).astype(jnp.int32)
    bf16, f32 = jnp.bfloat16, jnp.float32
    width = tensor * features
    slots = GROUPS * SLOTS
    pairs = SHARED * QUERIES
    same_core = [[chip * CORES + core for chip in range(CHIPS)] for core in range(CORES)]
    flip = [(g, g ^ 1) for g in range(GROUPS)]
    vmem = pl.BlockSpec(memory_space=VMEM)
    smem = pl.BlockSpec(memory_space=SMEM)
    hbm = pl.BlockSpec(memory_space=pltpu.HBM)
    shape = jax.ShapeDtypeStruct
    dma = pltpu.SemaphoreType.DMA

    tiles = features // WIDTH
    rows = tiles * TOKENS + 16
    spread = pl.pallas_call(
        spread_kernel,
        out_shape=pltpu.HBM((tensor, rows, WIDTH), bf16),
        in_specs=[hbm, hbm],
        out_specs=hbm,
        scratch_shapes=[
            VMEM(hidden.shape, bf16), VMEM((tiles, WIDTH), bf16), VMEM((rows, WIDTH), bf16),
            dma((2 + tensor,)),
        ],
        compiler_params=limit(SPREAD_MIB),
        name="spread",
    )(hidden, norm_gain.reshape(tiles, WIDTH))
    gathered = lax.all_to_all(spread, "tp", split_axis=0, concat_axis=0, tiled=True)

    lengths = lax.dynamic_slice_in_dim(cache_len, me * ROWS, ROWS)
    positions = (lengths[:, None] + jnp.arange(STEPS, dtype=jnp.int32)[None, :]).reshape(-1, 1)
    frequency = jnp.exp(
        jnp.arange(WIDTH // 2, dtype=f32) * (-2.0 * math.log(ROPE_BASE) / WIDTH)
    )
    angles = positions.astype(f32) * frequency[None, :]
    rows_flat = page_row.reshape(-1)
    seqs_flat = page_seq.reshape(-1)
    page_shape = (CHIPS, CORES, SLOTS, WIDTH, WIDTH)
    moved = (2, CHIPS, SLOTS, WIDTH, WIDTH)
    turns, caps, keep, give = pl.pallas_call(
        table_kernel,
        out_shape=(
            shape((4, TOKENS, WIDTH), f32), shape((slots // 8, WIDTH), jnp.int32),
            pltpu.HBM(moved, bf16), pltpu.HBM(moved, bf16),
        ),
        in_specs=[vmem] * 4 + [hbm] * 2 + [smem] * 4,
        out_specs=(vmem, vmem, hbm, hbm),
        scratch_shapes=[dma((4,))],
        compiler_params=limit(TABLE_MIB),
        cost_estimate=cost(TABLE_COST),
        name="tables",
    )(
        jnp.cos(angles), jnp.sin(angles), query_gain[None, :], key_gain[None, :],
        cache_keys.reshape(page_shape), cached_value_pages.reshape(page_shape),
        cache_len, rows_flat, seqs_flat, mine,
    )
    got = lax.ppermute(give, "dp", flip)
    send_q, pack, normed = pl.pallas_call(
        project_kernel,
        out_shape=(
            VMEM((CHIPS, pairs, WIDTH), bf16),
            shape((ROWS, QUERIES, WIDTH), bf16),
            pltpu.HBM((TOKENS, width), bf16),
        ),
        in_specs=[vmem] * 3 + [smem, hbm],
        out_specs=(vmem, vmem, hbm),
        scratch_shapes=[
            VMEM((TOKENS, width), bf16),
            SMEM((rows_flat.size,), jnp.int32), dma((2 + tensor // 2,)),
        ],
        compiler_params=limit(PROJECT_MIB),
        cost_estimate=cost(PROJECT_COST),
        name="project",
    )(gathered, w_query, turns, mine, rows_flat)
    got_q = lax.all_to_all(
        send_q, "dp", split_axis=0, concat_axis=0, tiled=True, axis_index_groups=same_core
    )
    new_key, new_value, new_max, new_total, new_out = pl.pallas_call(
        fresh_kernel,
        out_shape=(shape((TOKENS, WIDTH), bf16),) * 2
        + (shape((ROWS * QUERIES, WIDTH), f32),) * 3,
        in_specs=[vmem] * 5,
        out_specs=(vmem,) * 5,
        compiler_params=limit(FRESH_MIB),
        cost_estimate=cost(FRESH_COST),
        name="fresh",
    )(normed, key_projection, value_projection, turns, pack)
    send_out = pl.pallas_call(
        page_kernel,
        out_shape=pltpu.HBM((CHIPS, pairs + SIDE, WIDTH), bf16),
        in_specs=[vmem] * 4,
        out_specs=hbm,
        scratch_shapes=[
            VMEM((CHIPS, pairs + SIDE, WIDTH), bf16),
            VMEM((slots * QUERIES, WIDTH), f32),
            VMEM((slots * QUERIES, WIDTH), bf16),
            dma((1,)),
        ],
        compiler_params=limit(PAGES_MIB),
        name="pages",
    )(
        got_q, keep, got, caps,
    )
    got_out = lax.all_to_all(
        send_out, "dp", split_axis=0, concat_axis=0, tiled=True, axis_index_groups=same_core
    )
    attention = pl.pallas_call(
        combine_kernel,
        out_shape=shape((ROWS, STEPS, HEADS * WIDTH), bf16),
        in_specs=[vmem] * 4 + [smem] + [hbm] * 3,
        out_specs=vmem,
        scratch_shapes=[
            VMEM((slots + 1, QUERIES, WIDTH), f32),
            VMEM((slots + 1, QUERIES, WIDTH), f32),
            SMEM((slots + 8,), jnp.int32),
            SMEM((rows_flat.size,), jnp.int32),
            SMEM((seqs_flat.size,), jnp.int32),
            SMEM((ROWS,), jnp.int32),
            dma((3,)),
        ],
        compiler_params=limit(COMBINE_MIB),
        name="combine",
    )(got_out, new_max, new_total, new_out, mine, rows_flat, seqs_flat, remaining)
    return (
        attention,
        new_key.reshape(ROWS, STEPS, WIDTH),
        new_value.reshape(ROWS, STEPS, WIDTH),
    )


def solution(mesh):
    in_specs = (
        P("dp", None, "tp"),
        P("tp"),
        P(None, "tp"),
        P(None, "tp"),
        P(None, "tp"),
        P(),
        P(),
        P("dp", None, None, None, "tp"),
        P("dp", None, None, None, "tp"),
        P(),
        P("dp"),
        P(),
        P(),
    )
    out_specs = (P("dp", None, "tp"), P("dp", None, "tp"), P("dp", None, "tp"))
    return jax.shard_map(shards, mesh=mesh, in_specs=in_specs, out_specs=out_specs, check_vma=False)
```

```python
import functools
import math

import jax
import jax.numpy as jnp
from jax import lax
from jax.experimental import pallas as pl
from jax.experimental.pallas import tpu as pltpu
from jax.sharding import PartitionSpec as P

EPSILON = 1e-06
ROPE_BASE = 1000000.0
MASKED = -1e30
ROWS = 32
STEPS = 4
HEADS = 4
QUERIES = HEADS * STEPS
WIDTH = 128
GROUPS = 32
CORES = 2
CHIPS = GROUPS // CORES
SLOTS = 2
SHARED = CORES * SLOTS
TOKENS = ROWS * STEPS
SIDE = 8
SCALE = 1.0 / math.sqrt(WIDTH)

VMEM = pltpu.VMEM
SMEM = pltpu.SMEM


def slot_row(row_ref, holder, owner, c):
    return row_ref[(holder * GROUPS + owner) * SLOTS + c]


def spread_kernel(hidden_hbm, gain_hbm, out_ref, hidden_ref, gain_ref, block_ref, sem):
    features = hidden_hbm.shape[2]
    copies = [
        pltpu.make_async_copy(hidden_hbm, hidden_ref, sem.at[0]),
        pltpu.make_async_copy(gain_hbm, gain_ref, sem.at[1]),
    ]
    for copy in copies:
        copy.start()
    for copy in copies:
        copy.wait()
    tiles = features // WIDTH
    for i in range(0, ROWS, 4):
        part = [hidden_ref[i + k].astype(jnp.float32) for k in range(4)]
        part = jnp.concatenate(part, axis=0).astype(jnp.bfloat16)
        for f in range(tiles):
            first = f * TOKENS + i * STEPS
            block_ref[first : first + 4 * STEPS, :] = part[:, f * WIDTH : (f + 1) * WIDTH]
    gain = gain_ref[...].astype(jnp.float32)
    gain = jnp.concatenate([gain, jnp.zeros((16 - tiles, WIDTH), jnp.float32)], axis=0)
    block_ref[tiles * TOKENS : tiles * TOKENS + 16, :] = gain.astype(jnp.bfloat16)
    copies = [
        pltpu.make_async_copy(block_ref, out_ref.at[t], sem.at[2 + t])
        for t in range(out_ref.shape[0])
    ]
    for copy in copies:
        copy.start()
    for copy in copies:
        copy.wait()


def table_kernel(
    key_hbm, value_hbm, len_ref, row_ref, seq_ref, turn_out, cap_out, keep_hbm, give_hbm, sem
):
    me = lax.axis_index("dp")
    core = lax.rem(me, CORES)
    copies = []
    for n, pages in enumerate((key_hbm, value_hbm)):
        copies.append(pltpu.make_async_copy(pages.at[:, core], keep_hbm.at[n], sem.at[2 * n]))
        copies.append(
            pltpu.make_async_copy(pages.at[:, 1 - core], give_hbm.at[n], sem.at[2 * n + 1])
        )
    for copy in copies:
        copy.start()
    row = lax.broadcasted_iota(jnp.int32, (TOKENS, WIDTH), 0)
    position = row & (STEPS - 1)
    for r in range(ROWS):
        position = position + jnp.where(row // STEPS == r, len_ref[me * ROWS + r], 0)
    column = lax.broadcasted_iota(jnp.int32, (TOKENS, WIDTH), 1)
    half = (column & (WIDTH // 2 - 1)).astype(jnp.float32)
    angle = position.astype(jnp.float32) * jnp.exp(half * (-2.0 * math.log(ROPE_BASE) / WIDTH))
    turn_out[...] = jnp.where(column < WIDTH // 2, jnp.cos(angle), jnp.sin(angle))
    lane = lax.broadcasted_iota(jnp.int32, (1, WIDTH), 1) // QUERIES
    for j in range(GROUPS * SLOTS // 8):
        cap = jnp.zeros((1, WIDTH), jnp.int32)
        for i in range(8):
            chip, k, c = 2 * j + i // SHARED, i // SLOTS % CORES, i % SLOTS
            owner = chip * CORES + core
            holder = me if k == 0 else me + 1 - 2 * core
            place = (holder * GROUPS + owner) * SLOTS + c
            row = row_ref[place]
            length = len_ref[owner * ROWS + jnp.minimum(row, ROWS - 1)]
            cap = jnp.where(
                lane == i, jnp.where(row < ROWS, length - seq_ref[place] * WIDTH, 0), cap
            )
        cap_out[j : j + 1, :] = cap
    for copy in copies:
        copy.wait()


def unpacked(turn):
    other = pltpu.roll(turn, WIDTH // 2, 1)
    left = lax.broadcasted_iota(jnp.int32, turn.shape, 1) < WIDTH // 2
    return jnp.where(left, turn, other), jnp.where(left, -other, turn)


def rotated(heads, gain, cos, sin):
    mean = jnp.sum(heads * heads, axis=1, keepdims=True) * (1.0 / WIDTH)
    scaled = heads * lax.rsqrt(mean + EPSILON) * gain
    return scaled * cos + pltpu.roll(scaled, WIDTH // 2, 1) * sin


def project_kernel(
    x_ref, wq_ref, qg_ref, turn_ref, row_hbm,
    send_ref, pack_ref, norm_hbm, norm_ref, row_ref, sem,
):
    rows_copy = pltpu.make_async_copy(row_hbm, row_ref, sem.at[0])
    rows_copy.start()
    count = x_ref.shape[0]
    tiles = wq_ref.shape[0] // count // WIDTH

    def block(n):
        t, f = n // tiles, n % tiles
        return x_ref[t, f * TOKENS : (f + 1) * TOKENS, :].astype(jnp.float32)

    total = jnp.zeros((TOKENS, WIDTH), jnp.float32)
    for n in range(count * tiles):
        x = block(n)
        total = total + x * x
    total = jnp.sum(total, axis=1, keepdims=True)
    rstd = lax.rsqrt(total * (1.0 / (count * tiles * WIDTH)) + EPSILON)
    queries = jnp.zeros((TOKENS, HEADS * WIDTH), jnp.float32)
    chunk = 2 * tiles
    copies = []
    for s in range(0, count * tiles, chunk):
        parts = []
        for n in range(s, s + chunk):
            t, f = n // tiles, n % tiles
            last = tiles * TOKENS
            gain = x_ref[t, last : last + 16, :].astype(jnp.float32)[f : f + 1]
            parts.append((block(n) * rstd * gain).astype(jnp.bfloat16))
        part = jnp.concatenate(parts, axis=1)
        span = slice(s * WIDTH, (s + chunk) * WIDTH)
        norm_ref[:, span] = part
        copies.append(
            pltpu.make_async_copy(
                norm_ref.at[:, span], norm_hbm.at[:, span], sem.at[1 + s // chunk]
            )
        )
        copies[-1].start()
        queries += jnp.dot(part, wq_ref[span, :], preferred_element_type=jnp.float32)
    cos, sin = unpacked(turn_ref[...])
    q_gain = qg_ref[...].astype(jnp.float32)
    low = lax.broadcasted_iota(jnp.int32, (8, WIDTH), 0) < STEPS
    turned = [
        rotated(queries[:, h * WIDTH : (h + 1) * WIDTH], q_gain, cos, sin)
        for h in range(HEADS)
    ]
    for i in range(ROWS // 2):
        parts = [turned[h][8 * i : 8 * i + 8] for h in range(HEADS)]
        rolled = [pltpu.roll(p, STEPS, 0) for p in parts]
        even = [jnp.where(low, parts[h], rolled[h + 1]) for h in (0, 2)]
        odd = [jnp.where(low, rolled[h], parts[h + 1]) for h in (0, 2)]
        pack_ref[2 * i] = jnp.concatenate(even, axis=0).astype(jnp.bfloat16)
        pack_ref[2 * i + 1] = jnp.concatenate(odd, axis=0).astype(jnp.bfloat16)
    me = lax.axis_index("dp")
    rows_copy.wait()
    core = lax.rem(me, CORES)
    for chip in range(CHIPS):
        for k in range(CORES):
            holder = chip * CORES + (core if k == 0 else 1 - core)
            for c in range(SLOTS):
                row = jnp.minimum(slot_row(row_ref, holder, me, c), ROWS - 1)
                first = (k * SLOTS + c) * QUERIES
                send_ref[chip, first : first + QUERIES, :] = pack_ref[row]
    for copy in copies:
        copy.wait()


def fresh_kernel(
    norm_ref, wk_ref, wv_ref, kg_ref, turn_ref, pack_ref,
    key_ref, value_ref, max_ref, total_ref, out_ref,
):
    count = ROWS * QUERIES
    normed = norm_ref[...]
    keys = jnp.dot(normed, wk_ref[...], preferred_element_type=jnp.float32)
    keys = rotated(
        keys, kg_ref[...].astype(jnp.float32), *unpacked(turn_ref[...])
    ).astype(jnp.bfloat16)
    values = jnp.dot(normed, wv_ref[...], preferred_element_type=jnp.float32)
    values = values.astype(jnp.bfloat16)
    key_ref[...] = keys
    value_ref[...] = values
    scores = (
        lax.dot_general(
            pack_ref[...].reshape(count, WIDTH), keys,
            (((1,), (1,)), ((), ())), preferred_element_type=jnp.float32,
        )
        * SCALE
    )
    query = lax.broadcasted_iota(jnp.int32, (count, TOKENS), 0)
    token = lax.broadcasted_iota(jnp.int32, (count, TOKENS), 1)
    usable = ((query >> 4) == (token >> 2)) & ((token & 3) <= (query & 3))
    scores = jnp.where(usable, scores, MASKED)
    top = jnp.max(scores, axis=1, keepdims=True)
    weights = jnp.where(usable, jnp.exp(scores - top), 0.0).astype(jnp.bfloat16)
    total = jnp.sum(weights.astype(jnp.float32), axis=1, keepdims=True)
    out_ref[...] = jnp.dot(weights, values, preferred_element_type=jnp.float32)
    max_ref[...] = jnp.broadcast_to(top, (count, WIDTH))
    total_ref[...] = jnp.broadcast_to(total, (count, WIDTH))


def in_pieces(x):
    high = x.astype(jnp.bfloat16).astype(jnp.float32)
    rest = x - high
    middle = rest.astype(jnp.bfloat16).astype(jnp.float32)
    return [high, middle, rest - middle]


def page_kernel(
    q_ref, keep_ref, got_ref, cap_ref, send_hbm, send_ref, score_ref, weight_ref, sem
):
    token = lax.broadcasted_iota(jnp.int32, (WIDTH, WIDTH), 0)
    member = lax.broadcasted_iota(jnp.int32, (WIDTH, WIDTH), 1) // QUERIES
    side_row = lax.broadcasted_iota(jnp.int32, (SIDE, WIDTH), 0)
    batches = GROUPS * SLOTS // 8
    pairs = SHARED * QUERIES

    def page(n, slot):
        chip, k, c = slot // SHARED, slot // SLOTS % CORES, slot % SLOTS
        return (keep_ref if k == 0 else got_ref)[n, chip, c]

    zero = jnp.zeros((), jnp.bfloat16)
    for j in range(batches):
        queries = q_ref[2 * j : 2 * j + 2].reshape(WIDTH, WIDTH)
        turned = queries.astype(jnp.float32).T.astype(jnp.bfloat16)
        keys = jnp.concatenate([page(0, 8 * j + i) for i in range(8)], axis=1)
        spread = jnp.concatenate([jnp.where(member == i, turned, zero) for i in range(8)], axis=0)
        scores = jnp.dot(keys, spread, preferred_element_type=jnp.float32) * SCALE
        score_ref[j * WIDTH : (j + 1) * WIDTH, :] = jnp.where(
            token < cap_ref[j : j + 1, :], scores, MASKED
        )
    for j in range(batches):
        scores = score_ref[j * WIDTH : (j + 1) * WIDTH, :]
        top = jnp.max(scores, axis=0, keepdims=True)
        weights = jnp.exp(scores - top).astype(jnp.bfloat16).astype(jnp.float32)
        total = jnp.sum(weights, axis=0, keepdims=True)
        weight_ref[j * WIDTH : (j + 1) * WIDTH, :] = weights.T.astype(jnp.bfloat16)
        tile = jnp.zeros((SIDE, WIDTH), jnp.float32)
        for n, piece in enumerate(in_pieces(top) + in_pieces(total)):
            tile = jnp.where(side_row == n, piece, tile)
        for k in range(2):
            send_ref[2 * j + k, pairs : pairs + SIDE, :] = tile.astype(jnp.bfloat16)
    for slot in range(GROUPS * SLOTS):
        out = jnp.dot(
            weight_ref[slot * QUERIES : (slot + 1) * QUERIES, :], page(1, slot),
            preferred_element_type=jnp.float32,
        )
        c = slot % SHARED
        send_ref[slot // SHARED, c * QUERIES : (c + 1) * QUERIES, :] = out.astype(jnp.bfloat16)
    send = pltpu.make_async_copy(send_ref, send_hbm, sem.at[0])
    send.start()
    send.wait()


def combine_kernel(
    got_ref, max_ref, total_ref, out_ref, row_hbm, seq_hbm, remaining_hbm,
    attention_ref, top_wide, total_wide, index_ref, row_ref, seq_ref, remaining_ref, sem,
):
    copies = [
        pltpu.make_async_copy(row_hbm, row_ref, sem.at[0]),
        pltpu.make_async_copy(seq_hbm, seq_ref, sem.at[1]),
        pltpu.make_async_copy(remaining_hbm, remaining_ref, sem.at[2]),
    ]
    for copy in copies:
        copy.start()
    me = lax.axis_index("dp")
    core = lax.rem(me, CORES)
    pairs = SHARED * QUERIES
    none = GROUPS * SLOTS
    for i in range(ROWS * SLOTS):
        index_ref[i] = none
    sub = lax.broadcasted_iota(jnp.int32, (8, WIDTH), 0)
    tops, totals = [], []
    for b in range(CHIPS // 8):
        top_block = jnp.zeros((8, WIDTH), jnp.float32)
        total_block = jnp.zeros((8, WIDTH), jnp.float32)
        for i in range(8):
            tile = got_ref[8 * b + i, pairs : pairs + SIDE, :].astype(jnp.float32)
            top_block = jnp.where(sub == i, tile[0:1] + tile[1:2] + tile[2:3], top_block)
            total_block = jnp.where(sub == i, tile[3:4] + tile[4:5] + tile[5:6], total_block)
        tops.append(top_block)
        totals.append(total_block)
    side = jnp.concatenate(
        tops + totals + [jnp.zeros((WIDTH - 2 * CHIPS, WIDTH), jnp.float32)], axis=0
    )
    side = pltpu.roll(side, lax.rem((2 - lax.rem(me // CORES, 2)) * pairs, WIDTH), 1).T
    for chip in range(CHIPS):
        for c in range(SHARED):
            span = slice(c * QUERIES, (c + 1) * QUERIES)
            slot = chip * SHARED + c
            top_wide[slot] = jnp.broadcast_to(side[span, chip : chip + 1], (QUERIES, WIDTH))
            total_wide[slot] = jnp.broadcast_to(
                side[span, CHIPS + chip : CHIPS + chip + 1], (QUERIES, WIDTH)
            )
    top_wide[none] = jnp.full((QUERIES, WIDTH), MASKED, jnp.float32)
    total_wide[none] = jnp.zeros((QUERIES, WIDTH), jnp.float32)
    for copy in copies:
        copy.wait()
    for chip in range(CHIPS):
        for c in range(SHARED):
            holder = chip * CORES + (core if c < SLOTS else 1 - core)
            place = (holder * GROUPS + me) * SLOTS + c % SLOTS
            row = row_ref[place]
            index_ref[jnp.where(row < ROWS, row * SLOTS + seq_ref[place], none)] = (
                chip * SHARED + c
            )
    step = lax.broadcasted_iota(jnp.int32, (QUERIES, WIDTH), 0) & (STEPS - 1)
    for r in range(ROWS):
        span = slice(r * QUERIES, (r + 1) * QUERIES)
        tops, totals, outs = [max_ref[span, :]], [total_ref[span, :]], [out_ref[span, :]]
        for k in range(SLOTS):
            slot = index_ref[r * SLOTS + k]
            tops.append(top_wide[slot])
            totals.append(total_wide[slot])
            known = jnp.minimum(slot, none - 1)
            start = pl.multiple_of((known & (SHARED - 1)) * QUERIES, QUERIES)
            outs.append(got_ref[known >> 2, pl.ds(start, QUERIES), :].astype(jnp.float32))
        top = functools.reduce(jnp.maximum, tops)
        factors = [jnp.exp(t - top) for t in tops]
        above = sum(f * o for f, o in zip(factors, outs))
        below = sum(f * t for f, t in zip(factors, totals))
        result = jnp.where(step < remaining_ref[r], above / below, 0.0).astype(jnp.bfloat16)
        for h in range(HEADS):
            attention_ref[r, :, h * WIDTH : (h + 1) * WIDTH] = result[
                h * STEPS : (h + 1) * STEPS, :
            ]


SPREAD_MIB = 60
TABLE_MIB = 4
PROJECT_MIB = 8
FRESH_MIB = 8
PAGES_MIB = 6
COMBINE_MIB = 6
TABLE_COST = 20
PROJECT_COST = 10
FRESH_COST = 10


def limit(mib):
    return pltpu.CompilerParams(vmem_limit_bytes=mib * 1024 * 1024)


def cost(us):
    return pl.CostEstimate(flops=us << 30, bytes_accessed=1 << 20, transcendentals=0)


def shards(
    hidden, norm_gain, w_query, key_projection, value_projection, query_gain, key_gain,
    cache_keys, cached_value_pages, cache_len, remaining, page_row, page_seq,
):
    features = hidden.shape[2]
    tensor = lax.axis_size("tp")
    bf16, f32 = jnp.bfloat16, jnp.float32
    width = tensor * features
    slots = GROUPS * SLOTS
    pairs = SHARED * QUERIES
    same_core = [[chip * CORES + core for chip in range(CHIPS)] for core in range(CORES)]
    flip = [(g, g ^ 1) for g in range(GROUPS)]
    vmem = pl.BlockSpec(memory_space=VMEM)
    smem = pl.BlockSpec(memory_space=SMEM)
    hbm = pl.BlockSpec(memory_space=pltpu.HBM)
    shape = jax.ShapeDtypeStruct
    dma = pltpu.SemaphoreType.DMA

    tiles = features // WIDTH
    rows = tiles * TOKENS + 16
    spread = pl.pallas_call(
        spread_kernel,
        out_shape=pltpu.HBM((tensor, rows, WIDTH), bf16),
        in_specs=[hbm, hbm],
        out_specs=hbm,
        scratch_shapes=[
            VMEM(hidden.shape, bf16), VMEM((tiles, WIDTH), bf16), VMEM((rows, WIDTH), bf16),
            dma((2 + tensor,)),
        ],
        compiler_params=limit(SPREAD_MIB),
        name="spread",
    )(hidden, norm_gain.reshape(tiles, WIDTH))
    gathered = lax.all_to_all(spread, "tp", split_axis=0, concat_axis=0, tiled=True)

    rows_flat = page_row.reshape(-1)
    seqs_flat = page_seq.reshape(-1)
    page_shape = (CHIPS, CORES, SLOTS, WIDTH, WIDTH)
    moved = (2, CHIPS, SLOTS, WIDTH, WIDTH)
    turns, caps, keep, give = pl.pallas_call(
        table_kernel,
        out_shape=(
            shape((TOKENS, WIDTH), f32), shape((slots // 8, WIDTH), jnp.int32),
            pltpu.HBM(moved, bf16), pltpu.HBM(moved, bf16),
        ),
        in_specs=[hbm] * 2 + [smem] * 3,
        out_specs=(vmem, vmem, hbm, hbm),
        scratch_shapes=[dma((4,))],
        compiler_params=limit(TABLE_MIB),
        cost_estimate=cost(TABLE_COST),
        name="tables",
    )(
        cache_keys.reshape(page_shape), cached_value_pages.reshape(page_shape),
        cache_len, rows_flat, seqs_flat,
    )
    got = lax.ppermute(give, "dp", flip)
    send_q, pack, normed = pl.pallas_call(
        project_kernel,
        out_shape=(
            VMEM((CHIPS, pairs, WIDTH), bf16),
            shape((ROWS, QUERIES, WIDTH), bf16),
            pltpu.HBM((TOKENS, width), bf16),
        ),
        in_specs=[vmem] * 4 + [hbm],
        out_specs=(vmem, vmem, hbm),
        scratch_shapes=[
            VMEM((TOKENS, width), bf16),
            SMEM((rows_flat.size,), jnp.int32), dma((1 + tensor // 2,)),
        ],
        compiler_params=limit(PROJECT_MIB),
        cost_estimate=cost(PROJECT_COST),
        name="project",
    )(gathered, w_query, query_gain[None, :], turns, rows_flat)
    got_q = lax.all_to_all(
        send_q, "dp", split_axis=0, concat_axis=0, tiled=True, axis_index_groups=same_core
    )
    new_key, new_value, new_max, new_total, new_out = pl.pallas_call(
        fresh_kernel,
        out_shape=(shape((TOKENS, WIDTH), bf16),) * 2
        + (shape((ROWS * QUERIES, WIDTH), f32),) * 3,
        in_specs=[vmem] * 6,
        out_specs=(vmem,) * 5,
        compiler_params=limit(FRESH_MIB),
        cost_estimate=cost(FRESH_COST),
        name="fresh",
    )(normed, key_projection, value_projection, key_gain[None, :], turns, pack)
    send_out = pl.pallas_call(
        page_kernel,
        out_shape=pltpu.HBM((CHIPS, pairs + SIDE, WIDTH), bf16),
        in_specs=[vmem] * 4,
        out_specs=hbm,
        scratch_shapes=[
            VMEM((CHIPS, pairs + SIDE, WIDTH), bf16),
            VMEM((slots * QUERIES, WIDTH), f32),
            VMEM((slots * QUERIES, WIDTH), bf16),
            dma((1,)),
        ],
        compiler_params=limit(PAGES_MIB),
        name="pages",
    )(
        got_q, keep, got, caps,
    )
    got_out = lax.all_to_all(
        send_out, "dp", split_axis=0, concat_axis=0, tiled=True, axis_index_groups=same_core
    )
    attention = pl.pallas_call(
        combine_kernel,
        out_shape=shape((ROWS, STEPS, HEADS * WIDTH), bf16),
        in_specs=[vmem] * 4 + [hbm] * 3,
        out_specs=vmem,
        scratch_shapes=[
            VMEM((slots + 1, QUERIES, WIDTH), f32),
            VMEM((slots + 1, QUERIES, WIDTH), f32),
            SMEM((slots + 8,), jnp.int32),
            SMEM((rows_flat.size,), jnp.int32),
            SMEM((seqs_flat.size,), jnp.int32),
            SMEM((ROWS,), jnp.int32),
            dma((3,)),
        ],
        compiler_params=limit(COMBINE_MIB),
        name="combine",
    )(got_out, new_max, new_total, new_out, rows_flat, seqs_flat, remaining)
    return (
        attention,
        new_key.reshape(ROWS, STEPS, WIDTH),
        new_value.reshape(ROWS, STEPS, WIDTH),
    )


def solution(mesh):
    in_specs = (
        P("dp", None, "tp"),
        P("tp"),
        P(None, "tp"),
        P(None, "tp"),
        P(None, "tp"),
        P(),
        P(),
        P("dp", None, None, None, "tp"),
        P("dp", None, None, None, "tp"),
        P(),
        P("dp"),
        P(),
        P(),
    )
    out_specs = (P("dp", None, "tp"), P("dp", None, "tp"), P("dp", None, "tp"))
    return jax.shard_map(shards, mesh=mesh, in_specs=in_specs, out_specs=out_specs, check_vma=False)
```

```python
import functools
import math

import jax
import jax.numpy as jnp
from jax import lax
from jax.experimental import pallas as pl
from jax.experimental.pallas import tpu as pltpu
from jax.sharding import PartitionSpec as P

EPSILON = 1e-06
ROPE_BASE = 1000000.0
MASKED = -1e30
ROWS = 32
STEPS = 4
HEADS = 4
QUERIES = HEADS * STEPS
WIDTH = 128
GROUPS = 32
CORES = 2
CHIPS = GROUPS // CORES
SLOTS = 2
FIRST_LEFT = 96
INDEX = 1024
SHARED = CORES * SLOTS
TOKENS = ROWS * STEPS
SIDE = 8
SCALE = 1.0 / math.sqrt(WIDTH)

VMEM = pltpu.VMEM
SMEM = pltpu.SMEM


def spread_kernel(hidden_hbm, gain_hbm, out_ref, hidden_ref, gain_ref, block_ref, sem):
    features = hidden_hbm.shape[2]
    copies = [
        pltpu.make_async_copy(hidden_hbm, hidden_ref, sem.at[0]),
        pltpu.make_async_copy(gain_hbm, gain_ref, sem.at[1]),
    ]
    for copy in copies:
        copy.start()
    for copy in copies:
        copy.wait()
    tiles = features // WIDTH
    for i in range(0, ROWS, 4):
        part = [hidden_ref[i + k].astype(jnp.float32) for k in range(4)]
        part = jnp.concatenate(part, axis=0).astype(jnp.bfloat16)
        for f in range(tiles):
            first = f * TOKENS + i * STEPS
            block_ref[first : first + 4 * STEPS, :] = part[:, f * WIDTH : (f + 1) * WIDTH]
    gain = gain_ref[...].astype(jnp.float32)
    gain = jnp.concatenate([gain, jnp.zeros((16 - tiles, WIDTH), jnp.float32)], axis=0)
    block_ref[tiles * TOKENS : tiles * TOKENS + 16, :] = gain.astype(jnp.bfloat16)
    copies = [
        pltpu.make_async_copy(block_ref, out_ref.at[t], sem.at[2 + t])
        for t in range(out_ref.shape[0])
    ]
    for copy in copies:
        copy.start()
    for copy in copies:
        copy.wait()


def table_kernel(
    key_hbm, value_hbm, wq_hbm, len_ref, left_ref, row_ref, seq_ref,
    turn_out, cap_out, index_out, keep_hbm, give_hbm, *rest,
):
    parts, (index_ref, sem) = rest[:-2], rest[-2:]
    depth = parts[0].shape[0]
    me = lax.axis_index("dp")
    core = lax.rem(me, CORES)
    copies = [
        pltpu.make_async_copy(wq_hbm.at[n * depth : (n + 1) * depth], part, sem.at[4 + n])
        for n, part in enumerate(parts)
    ]
    for n, pages in enumerate((key_hbm, value_hbm)):
        copies.append(pltpu.make_async_copy(pages.at[:, core], keep_hbm.at[n], sem.at[2 * n]))
        copies.append(
            pltpu.make_async_copy(pages.at[:, 1 - core], give_hbm.at[n], sem.at[2 * n + 1])
        )
    for copy in copies:
        copy.start()
    row = lax.broadcasted_iota(jnp.int32, (TOKENS, WIDTH), 0)
    position = row & (STEPS - 1)
    for r in range(ROWS):
        position = position + jnp.where(row // STEPS == r, len_ref[me * ROWS + r], 0)
    column = lax.broadcasted_iota(jnp.int32, (TOKENS, WIDTH), 1)
    half = (column & (WIDTH // 2 - 1)).astype(jnp.float32)
    angle = position.astype(jnp.float32) * jnp.exp(half * (-2.0 * math.log(ROPE_BASE) / WIDTH))
    turn_out[...] = jnp.where(column < WIDTH // 2, jnp.cos(angle), jnp.sin(angle))
    lane = lax.broadcasted_iota(jnp.int32, (1, WIDTH), 1) // QUERIES
    for j in range(GROUPS * SLOTS // 8):
        cap = jnp.zeros((1, WIDTH), jnp.int32)
        for i in range(8):
            chip, k, c = 2 * j + i // SHARED, i // SLOTS % CORES, i % SLOTS
            owner = chip * CORES + core
            holder = me if k == 0 else me + 1 - 2 * core
            place = (holder * GROUPS + owner) * SLOTS + c
            row = row_ref[place]
            length = len_ref[owner * ROWS + jnp.minimum(row, ROWS - 1)]
            cap = jnp.where(
                lane == i, jnp.where(row < ROWS, length - seq_ref[place] * WIDTH, 0), cap
            )
        cap_out[j : j + 1, :] = cap
    none = GROUPS * SLOTS
    for i in range(none + 1):
        index_ref[i] = none
    for chip in range(CHIPS):
        for c in range(SHARED):
            holder = chip * CORES + (core if c < SLOTS else 1 - core)
            place = (holder * GROUPS + me) * SLOTS + c % SLOTS
            row = row_ref[place]
            slot = chip * SHARED + c
            index_ref[jnp.where(row < ROWS, row * SLOTS + seq_ref[place], none)] = slot
    for r in range(ROWS):
        index_ref[FIRST_LEFT + r] = left_ref[r]
    copies.append(pltpu.make_async_copy(index_ref, index_out, sem.at[4 + len(parts)]))
    copies[-1].start()
    for copy in copies:
        copy.wait()


def unpacked(turn):
    other = pltpu.roll(turn, WIDTH // 2, 1)
    left = lax.broadcasted_iota(jnp.int32, turn.shape, 1) < WIDTH // 2
    return jnp.where(left, turn, other), jnp.where(left, -other, turn)


def rotated(heads, gain, cos, sin):
    mean = jnp.sum(heads * heads, axis=1, keepdims=True) * (1.0 / WIDTH)
    scaled = heads * lax.rsqrt(mean + EPSILON) * gain
    return scaled * cos + pltpu.roll(scaled, WIDTH // 2, 1) * sin


def norm_kernel(x_ref, norm_ref):
    count = x_ref.shape[0]
    tiles = norm_ref.shape[1] // count // WIDTH

    def block(n):
        t, f = n // tiles, n % tiles
        return x_ref[t, f * TOKENS : (f + 1) * TOKENS, :].astype(jnp.float32)

    total = jnp.zeros((TOKENS, WIDTH), jnp.float32)
    for n in range(count * tiles):
        x = block(n)
        total = total + x * x
    total = jnp.sum(total, axis=1, keepdims=True)
    rstd = lax.rsqrt(total * (1.0 / (count * tiles * WIDTH)) + EPSILON)
    last = tiles * TOKENS
    for n in range(count * tiles):
        t, f = n // tiles, n % tiles
        gain = x_ref[t, last : last + 16, :].astype(jnp.float32)[f : f + 1]
        norm_ref[:, n * WIDTH : (n + 1) * WIDTH] = (block(n) * rstd * gain).astype(jnp.bfloat16)


def project_kernel(
    norm_ref, qg_ref, turn_ref, row_hbm, *rest,
):
    parts, (send_ref, pack_ref, norm_hbm, row_ref, sem) = rest[:-5], rest[-5:]
    copies = [pltpu.make_async_copy(norm_ref, norm_hbm, sem.at[1])]
    copies[0].start()
    rows_copy = pltpu.make_async_copy(row_hbm, row_ref, sem.at[0])
    rows_copy.start()
    depth = parts[0].shape[0]
    queries = sum(
        jnp.dot(
            norm_ref[:, n * depth : (n + 1) * depth], part[...],
            preferred_element_type=jnp.float32,
        )
        for n, part in enumerate(parts)
    )
    cos, sin = unpacked(turn_ref[...])
    q_gain = qg_ref[...].astype(jnp.float32)
    low = lax.broadcasted_iota(jnp.int32, (8, WIDTH), 0) < STEPS
    turned = [
        rotated(queries[:, h * WIDTH : (h + 1) * WIDTH], q_gain, cos, sin)
        for h in range(HEADS)
    ]
    for i in range(ROWS // 2):
        parts = [turned[h][8 * i : 8 * i + 8] for h in range(HEADS)]
        rolled = [pltpu.roll(p, STEPS, 0) for p in parts]
        even = [jnp.where(low, parts[h], rolled[h + 1]) for h in (0, 2)]
        odd = [jnp.where(low, rolled[h], parts[h + 1]) for h in (0, 2)]
        pack_ref[2 * i] = jnp.concatenate(even, axis=0).astype(jnp.bfloat16)
        pack_ref[2 * i + 1] = jnp.concatenate(odd, axis=0).astype(jnp.bfloat16)
    me = lax.axis_index("dp")
    core = lax.rem(me, CORES)
    rows_copy.wait()
    for chip in range(CHIPS):
        for c in range(SHARED):
            holder = chip * CORES + (core if c < SLOTS else 1 - core)
            place = (holder * GROUPS + me) * SLOTS + c % SLOTS
            row = jnp.minimum(row_ref[place], ROWS - 1)
            send_ref[chip, c * QUERIES : (c + 1) * QUERIES, :] = pack_ref[row]
    for copy in copies:
        copy.wait()


def fresh_kernel(
    norm_ref, wk_ref, wv_ref, kg_ref, turn_ref, pack_ref,
    key_ref, value_ref, max_ref, total_ref, out_ref,
):
    count = ROWS * QUERIES
    normed = norm_ref[...]
    keys = jnp.dot(normed, wk_ref[...], preferred_element_type=jnp.float32)
    keys = rotated(
        keys, kg_ref[...].astype(jnp.float32), *unpacked(turn_ref[...])
    ).astype(jnp.bfloat16)
    values = jnp.dot(normed, wv_ref[...], preferred_element_type=jnp.float32)
    values = values.astype(jnp.bfloat16)
    key_ref[...] = keys
    value_ref[...] = values
    scores = (
        lax.dot_general(
            pack_ref[...].reshape(count, WIDTH), keys,
            (((1,), (1,)), ((), ())), preferred_element_type=jnp.float32,
        )
        * SCALE
    )
    query = lax.broadcasted_iota(jnp.int32, (count, TOKENS), 0)
    token = lax.broadcasted_iota(jnp.int32, (count, TOKENS), 1)
    usable = ((query >> 4) == (token >> 2)) & ((token & 3) <= (query & 3))
    scores = jnp.where(usable, scores, MASKED)
    top = jnp.max(scores, axis=1, keepdims=True)
    weights = jnp.where(usable, jnp.exp(scores - top), 0.0).astype(jnp.bfloat16)
    total = jnp.sum(weights.astype(jnp.float32), axis=1, keepdims=True)
    out_ref[...] = jnp.dot(weights, values, preferred_element_type=jnp.float32)
    max_ref[...] = jnp.broadcast_to(top, (count, WIDTH))
    total_ref[...] = jnp.broadcast_to(total, (count, WIDTH))


def in_pieces(x):
    high = x.astype(jnp.bfloat16).astype(jnp.float32)
    rest = x - high
    middle = rest.astype(jnp.bfloat16).astype(jnp.float32)
    return [high, middle, rest - middle]


def page_kernel(
    q_ref, keep_ref, got_ref, cap_ref, send_ref, score_ref, weight_ref
):
    token = lax.broadcasted_iota(jnp.int32, (WIDTH, WIDTH), 0)
    member = lax.broadcasted_iota(jnp.int32, (WIDTH, WIDTH), 1) // QUERIES
    side_row = lax.broadcasted_iota(jnp.int32, (SIDE, WIDTH), 0)
    batches = GROUPS * SLOTS // 8
    pairs = SHARED * QUERIES

    def page(n, slot):
        chip, k, c = slot // SHARED, slot // SLOTS % CORES, slot % SLOTS
        return (keep_ref if k == 0 else got_ref)[n, chip, c]

    zero = jnp.zeros((), jnp.bfloat16)
    for j in range(batches):
        queries = q_ref[2 * j : 2 * j + 2].reshape(WIDTH, WIDTH)
        turned = queries.astype(jnp.float32).T.astype(jnp.bfloat16)
        keys = jnp.concatenate([page(0, 8 * j + i) for i in range(8)], axis=1)
        spread = jnp.concatenate([jnp.where(member == i, turned, zero) for i in range(8)], axis=0)
        scores = jnp.dot(keys, spread, preferred_element_type=jnp.float32) * SCALE
        score_ref[j * WIDTH : (j + 1) * WIDTH, :] = jnp.where(
            token < cap_ref[j : j + 1, :], scores, MASKED
        )
    for j in range(batches):
        scores = score_ref[j * WIDTH : (j + 1) * WIDTH, :]
        top = jnp.max(scores, axis=0, keepdims=True)
        weights = jnp.exp(scores - top).astype(jnp.bfloat16).astype(jnp.float32)
        total = jnp.sum(weights, axis=0, keepdims=True)
        weight_ref[j * WIDTH : (j + 1) * WIDTH, :] = weights.T.astype(jnp.bfloat16)
        tile = jnp.zeros((SIDE, WIDTH), jnp.float32)
        for n, piece in enumerate(in_pieces(top) + in_pieces(total)):
            tile = jnp.where(side_row == n, piece, tile)
        for k in range(2):
            send_ref[2 * j + k, pairs : pairs + SIDE, :] = tile.astype(jnp.bfloat16)
    for slot in range(0, GROUPS * SLOTS, 2):
        out = jnp.dot(
            weight_ref[slot * QUERIES : (slot + 2) * QUERIES, :],
            jnp.concatenate([page(1, slot), page(1, slot + 1)], axis=1),
            preferred_element_type=jnp.float32,
        )
        first = slot % SHARED * QUERIES
        out = jnp.concatenate([out[:QUERIES, :WIDTH], out[QUERIES:, WIDTH:]], axis=0)
        send_ref[slot // SHARED, first : first + 2 * QUERIES, :] = out.astype(jnp.bfloat16)


def combine_kernel(
    got_ref, max_ref, total_ref, out_ref, index_hbm,
    attention_hbm, attention_ref, top_wide, total_wide, index_ref, sem,
):
    index_copy = pltpu.make_async_copy(index_hbm, index_ref, sem.at[0])
    index_copy.start()
    me = lax.axis_index("dp")
    pairs = SHARED * QUERIES
    none = GROUPS * SLOTS
    sub = lax.broadcasted_iota(jnp.int32, (8, WIDTH), 0)
    tops, totals = [], []
    for b in range(CHIPS // 8):
        top_block = jnp.zeros((8, WIDTH), jnp.float32)
        total_block = jnp.zeros((8, WIDTH), jnp.float32)
        for i in range(8):
            tile = got_ref[8 * b + i, pairs : pairs + SIDE, :].astype(jnp.float32)
            top_block = jnp.where(sub == i, tile[0:1] + tile[1:2] + tile[2:3], top_block)
            total_block = jnp.where(sub == i, tile[3:4] + tile[4:5] + tile[5:6], total_block)
        tops.append(top_block)
        totals.append(total_block)
    side = jnp.concatenate(
        tops + totals + [jnp.zeros((WIDTH - 2 * CHIPS, WIDTH), jnp.float32)], axis=0
    )
    side = pltpu.roll(side, lax.rem((2 - lax.rem(me // CORES, 2)) * pairs, WIDTH), 1).T
    for chip in range(CHIPS):
        for c in range(SHARED):
            span = slice(c * QUERIES, (c + 1) * QUERIES)
            slot = chip * SHARED + c
            top_wide[slot] = jnp.broadcast_to(side[span, chip : chip + 1], (QUERIES, WIDTH))
            total_wide[slot] = jnp.broadcast_to(
                side[span, CHIPS + chip : CHIPS + chip + 1], (QUERIES, WIDTH)
            )
    top_wide[none] = jnp.full((QUERIES, WIDTH), MASKED, jnp.float32)
    total_wide[none] = jnp.zeros((QUERIES, WIDTH), jnp.float32)
    index_copy.wait()
    copies = []
    step = lax.broadcasted_iota(jnp.int32, (QUERIES, WIDTH), 0) & (STEPS - 1)
    for r in range(ROWS):
        span = slice(r * QUERIES, (r + 1) * QUERIES)
        tops, totals, outs = [max_ref[span, :]], [total_ref[span, :]], [out_ref[span, :]]
        for k in range(SLOTS):
            slot = index_ref[r * SLOTS + k]
            tops.append(top_wide[slot])
            totals.append(total_wide[slot])
            known = jnp.minimum(slot, none - 1)
            start = pl.multiple_of((known & (SHARED - 1)) * QUERIES, QUERIES)
            outs.append(got_ref[known >> 2, pl.ds(start, QUERIES), :].astype(jnp.float32))
        top = functools.reduce(jnp.maximum, tops)
        factors = [jnp.exp(t - top) for t in tops]
        above = sum(f * o for f, o in zip(factors, outs))
        below = sum(f * t for f, t in zip(factors, totals))
        result = jnp.where(step < index_ref[FIRST_LEFT + r], above / below, 0.0).astype(jnp.bfloat16)
        for h in range(HEADS):
            attention_ref[r, :, h * WIDTH : (h + 1) * WIDTH] = result[
                h * STEPS : (h + 1) * STEPS, :
            ]
        if r % 8 == 7:
            done = slice(r - 7, r + 1)
            copies.append(
                pltpu.make_async_copy(
                    attention_ref.at[done], attention_hbm.at[done], sem.at[1 + r // 8]
                )
            )
            copies[-1].start()
    for copy in copies:
        copy.wait()


SPREAD_MIB = 60
TABLE_MIB = 4
PARTS = 4
NORM_MIB = 4
NORM_COST = 20
PROJECT_MIB = 8
FRESH_MIB = 8
PAGES_MIB = 6
COMBINE_MIB = 6
TABLE_COST = 20
PROJECT_COST = 10
FRESH_COST = 10


def limit(mib):
    return pltpu.CompilerParams(vmem_limit_bytes=mib * 1024 * 1024)


def cost(us):
    return pl.CostEstimate(flops=us << 30, bytes_accessed=1 << 20, transcendentals=0)


def shards(
    hidden, norm_gain, w_query, key_projection, value_projection, query_gain, key_gain,
    cache_keys, cached_value_pages, cache_len, remaining, page_row, page_seq,
):
    features = hidden.shape[2]
    tensor = lax.axis_size("tp")
    bf16, f32 = jnp.bfloat16, jnp.float32
    width = tensor * features
    slots = GROUPS * SLOTS
    pairs = SHARED * QUERIES
    same_core = [[chip * CORES + core for chip in range(CHIPS)] for core in range(CORES)]
    flip = [(g, g ^ 1) for g in range(GROUPS)]
    vmem = pl.BlockSpec(memory_space=VMEM)
    smem = pl.BlockSpec(memory_space=SMEM)
    hbm = pl.BlockSpec(memory_space=pltpu.HBM)
    shape = jax.ShapeDtypeStruct
    dma = pltpu.SemaphoreType.DMA

    tiles = features // WIDTH
    rows = tiles * TOKENS + 16
    spread = pl.pallas_call(
        spread_kernel,
        out_shape=pltpu.HBM((tensor, rows, WIDTH), bf16),
        in_specs=[hbm, hbm],
        out_specs=hbm,
        scratch_shapes=[
            VMEM(hidden.shape, bf16), VMEM((tiles, WIDTH), bf16), VMEM((rows, WIDTH), bf16),
            dma((2 + tensor,)),
        ],
        compiler_params=limit(SPREAD_MIB),
        name="spread",
    )(hidden, norm_gain.reshape(tiles, WIDTH))
    gathered = lax.all_to_all(spread, "tp", split_axis=0, concat_axis=0, tiled=True)

    rows_flat = page_row.reshape(-1)
    seqs_flat = page_seq.reshape(-1)
    page_shape = (CHIPS, CORES, SLOTS, WIDTH, WIDTH)
    moved = (2, CHIPS, SLOTS, WIDTH, WIDTH)
    turns, caps, index, keep, give, *weights = pl.pallas_call(
        table_kernel,
        out_shape=(
            shape((TOKENS, WIDTH), f32), shape((slots // 8, WIDTH), jnp.int32),
            VMEM((INDEX,), jnp.int32),
            pltpu.HBM(moved, bf16), pltpu.HBM(moved, bf16),
        )
        + (pltpu.HBM((width // PARTS, HEADS * WIDTH), bf16),) * PARTS,
        in_specs=[hbm] * 3 + [smem] * 4,
        out_specs=(vmem, vmem, vmem) + (hbm,) * (2 + PARTS),
        scratch_shapes=[SMEM((INDEX,), jnp.int32), dma((5 + PARTS,))],
        compiler_params=limit(TABLE_MIB),
        cost_estimate=cost(TABLE_COST),
        name="tables",
    )(
        cache_keys.reshape(page_shape), cached_value_pages.reshape(page_shape),
        w_query, cache_len, remaining, rows_flat, seqs_flat,
    )
    got = lax.ppermute(give, "dp", flip)
    states = pl.pallas_call(
        norm_kernel,
        out_shape=VMEM((TOKENS, width), bf16),
        in_specs=[vmem],
        out_specs=vmem,
        compiler_params=limit(NORM_MIB),
        cost_estimate=cost(NORM_COST),
        name="normalise",
    )(gathered)
    send_q, pack, normed = pl.pallas_call(
        project_kernel,
        out_shape=(
            VMEM((CHIPS, pairs, WIDTH), bf16),
            shape((ROWS, QUERIES, WIDTH), bf16),
            pltpu.HBM((TOKENS, width), bf16),
        ),
        in_specs=[vmem] * 3 + [hbm] + [vmem] * PARTS,
        out_specs=(vmem, vmem, hbm),
        scratch_shapes=[SMEM((rows_flat.size,), jnp.int32), dma((2,))],
        compiler_params=limit(PROJECT_MIB),
        cost_estimate=cost(PROJECT_COST),
        name="project",
    )(states, query_gain[None, :], turns, rows_flat, *weights)
    got_q = lax.all_to_all(
        send_q, "dp", split_axis=0, concat_axis=0, tiled=True, axis_index_groups=same_core
    )
    new_key, new_value, new_max, new_total, new_out = pl.pallas_call(
        fresh_kernel,
        out_shape=(shape((TOKENS, WIDTH), bf16),) * 2
        + (shape((ROWS * QUERIES, WIDTH), f32),) * 3,
        in_specs=[vmem] * 6,
        out_specs=(vmem,) * 5,
        compiler_params=limit(FRESH_MIB),
        cost_estimate=cost(FRESH_COST),
        name="fresh",
    )(normed, key_projection, value_projection, key_gain[None, :], turns, pack)
    send_out = pl.pallas_call(
        page_kernel,
        out_shape=VMEM((CHIPS, pairs + SIDE, WIDTH), bf16),
        in_specs=[vmem] * 4,
        out_specs=vmem,
        scratch_shapes=[
            VMEM((slots * QUERIES, WIDTH), f32),
            VMEM((slots * QUERIES, WIDTH), bf16),
        ],
        compiler_params=limit(PAGES_MIB),
        name="pages",
    )(
        got_q, keep, got, caps,
    )
    got_out = lax.all_to_all(
        send_out, "dp", split_axis=0, concat_axis=0, tiled=True, axis_index_groups=same_core
    )
    attention = pl.pallas_call(
        combine_kernel,
        out_shape=pltpu.HBM((ROWS, STEPS, HEADS * WIDTH), bf16),
        in_specs=[vmem] * 4 + [hbm],
        out_specs=hbm,
        scratch_shapes=[
            VMEM((ROWS, STEPS, HEADS * WIDTH), bf16),
            VMEM((slots + 1, QUERIES, WIDTH), f32),
            VMEM((slots + 1, QUERIES, WIDTH), f32),
            SMEM((INDEX,), jnp.int32),
            dma((1 + ROWS // 8,)),
        ],
        compiler_params=limit(COMBINE_MIB),
        name="combine",
    )(got_out, new_max, new_total, new_out, index)
    return (
        attention,
        new_key.reshape(ROWS, STEPS, WIDTH),
        new_value.reshape(ROWS, STEPS, WIDTH),
    )


def solution(mesh):
    in_specs = (
        P("dp", None, "tp"),
        P("tp"),
        P(None, "tp"),
        P(None, "tp"),
        P(None, "tp"),
        P(),
        P(),
        P("dp", None, None, None, "tp"),
        P("dp", None, None, None, "tp"),
        P(),
        P("dp"),
        P(),
        P(),
    )
    out_specs = (P("dp", None, "tp"), P("dp", None, "tp"), P("dp", None, "tp"))
    return jax.shard_map(shards, mesh=mesh, in_specs=in_specs, out_specs=out_specs, check_vma=False)
```

```python
import functools
import math

import jax
import jax.numpy as jnp
from jax import lax
from jax.experimental import pallas as pl
from jax.experimental.pallas import tpu as pltpu
from jax.sharding import PartitionSpec as P

EPSILON = 1e-06
ROPE_BASE = 1000000.0
MASKED = -1e30
ROWS = 32
STEPS = 4
HEADS = 4
QUERIES = HEADS * STEPS
WIDTH = 128
GROUPS = 32
CORES = 2
CHIPS = GROUPS // CORES
SLOTS = 2
FIRST_LEFT = 96
FIRST_ROW = 128
INDEX = 1024
SHARDS = 8
CUT = 320
SHARED = CORES * SLOTS
TOKENS = ROWS * STEPS
SIDE = 8
SCALE = 1.0 / math.sqrt(WIDTH)

VMEM = pltpu.VMEM
SMEM = pltpu.SMEM


def block_kernel(hidden_hbm, gain_hbm, block_ref, hidden_ref, gain_ref, sem):
    copies = [
        pltpu.make_async_copy(hidden_hbm, hidden_ref, sem.at[0]),
        pltpu.make_async_copy(gain_hbm, gain_ref, sem.at[1]),
    ]
    for copy in copies:
        copy.start()
    for copy in copies:
        copy.wait()
    tiles = hidden_hbm.shape[2] // WIDTH
    for i in range(0, ROWS, 4):
        part = [hidden_ref[i + k].astype(jnp.float32) for k in range(4)]
        part = jnp.concatenate(part, axis=0).astype(jnp.bfloat16)
        for f in range(tiles):
            first = f * TOKENS + i * STEPS
            block_ref[first : first + 4 * STEPS, :] = part[:, f * WIDTH : (f + 1) * WIDTH]
    gain = gain_ref[...].astype(jnp.float32)
    gain = jnp.concatenate([gain, jnp.zeros((16 - tiles, WIDTH), jnp.float32)], axis=0)
    block_ref[tiles * TOKENS : tiles * TOKENS + 16, :] = gain.astype(jnp.bfloat16)


def table_kernel(
    key_hbm, value_hbm, len_hbm, left_hbm, row_hbm, seq_hbm,
    turn_out, cap_out, index_out, keep_hbm, give_hbm,
    stage_ref, index_ref, len_ref, left_ref, row_ref, seq_ref, sem,
):
    scalars = [
        pltpu.make_async_copy(source, target, sem.at[9 + n])
        for n, (source, target) in enumerate(
            ((len_hbm, len_ref), (left_hbm, left_ref), (row_hbm, row_ref), (seq_hbm, seq_ref))
        )
    ]
    for copy in scalars:
        copy.start()
    me = lax.axis_index("dp")
    core = lax.rem(me, CORES)
    arrivals, departures = [], []
    for target, half in ((give_hbm, 1 - core), (keep_hbm, core)):
        for n, pages in enumerate((key_hbm, value_hbm)):
            place = len(arrivals)
            staged = stage_ref.at[place]
            arrivals.append(pltpu.make_async_copy(pages.at[:, half], staged, sem.at[place]))
            departures.append(pltpu.make_async_copy(staged, target.at[n], sem.at[4 + place]))
    for copy in arrivals:
        copy.start()
    for copy in scalars:
        copy.wait()
    row = lax.broadcasted_iota(jnp.int32, (TOKENS, WIDTH), 0)
    position = row & (STEPS - 1)
    for r in range(ROWS):
        position = position + jnp.where(row // STEPS == r, len_ref[me * ROWS + r], 0)
    column = lax.broadcasted_iota(jnp.int32, (TOKENS, WIDTH), 1)
    half = (column & (WIDTH // 2 - 1)).astype(jnp.float32)
    angle = position.astype(jnp.float32) * jnp.exp(half * (-2.0 * math.log(ROPE_BASE) / WIDTH))
    turn_out[...] = jnp.where(column < WIDTH // 2, jnp.cos(angle), jnp.sin(angle))
    lane = lax.broadcasted_iota(jnp.int32, (1, WIDTH), 1) // QUERIES
    for j in range(GROUPS * SLOTS // 8):
        cap = jnp.zeros((1, WIDTH), jnp.int32)
        for i in range(8):
            chip, k, c = 2 * j + i // SHARED, i // SLOTS % CORES, i % SLOTS
            owner = chip * CORES + core
            holder = me if k == 0 else me + 1 - 2 * core
            row = row_ref[holder, c, owner]
            length = len_ref[owner * ROWS + jnp.minimum(row, ROWS - 1)]
            cap = jnp.where(
                lane == i, jnp.where(row < ROWS, length - seq_ref[holder, c, owner] * WIDTH, 0), cap
            )
        cap_out[j : j + 1, :] = cap
    for arrival, departure in zip(arrivals, departures):
        arrival.wait()
        departure.start()
    none = GROUPS * SLOTS
    for i in range(none + 1):
        index_ref[i] = none
    for chip in range(CHIPS):
        for c in range(SHARED):
            holder = chip * CORES + (core if c < SLOTS else 1 - core)
            row = row_ref[holder, c % SLOTS, me]
            seq = seq_ref[holder, c % SLOTS, me]
            slot = chip * SHARED + c
            index_ref[jnp.where(row < ROWS, row * SLOTS + seq, none)] = slot
            index_ref[FIRST_ROW + slot] = jnp.minimum(row, ROWS - 1)
    for r in range(ROWS):
        index_ref[FIRST_LEFT + r] = left_ref[r]
    index_copy = pltpu.make_async_copy(index_ref, index_out, sem.at[8])
    index_copy.start()
    for departure in departures:
        departure.wait()
    index_copy.wait()


def unpacked(turn):
    other = pltpu.roll(turn, WIDTH // 2, 1)
    left = lax.broadcasted_iota(jnp.int32, turn.shape, 1) < WIDTH // 2
    return jnp.where(left, turn, other), jnp.where(left, -other, turn)


def rotated(heads, gain, cos, sin):
    mean = jnp.sum(heads * heads, axis=1, keepdims=True) * (1.0 / WIDTH)
    scaled = heads * lax.rsqrt(mean + EPSILON) * gain
    return scaled * cos + pltpu.roll(scaled, WIDTH // 2, 1) * sin


def norm_kernel(*refs):
    shards, norm_ref = refs[:-1], refs[-1]
    count = SHARDS
    tiles = norm_ref.shape[1] // count // WIDTH
    pieces = {0: (0,), 1: (1,), 2: (2,), 3: (3,), 4: (4, 5), 5: (6, 7), 6: (8,), 7: (9,)}

    def rows(t, first, last):
        held = pieces[t]
        if len(held) == 1:
            return shards[held[0]][first:last, :].astype(jnp.float32)
        if last <= CUT:
            return shards[held[0]][first:last, :].astype(jnp.float32)
        if first >= CUT:
            return shards[held[1]][first - CUT : last - CUT, :].astype(jnp.float32)
        return jnp.concatenate([rows(t, first, CUT), rows(t, CUT, last)], axis=0)

    def block(n):
        t, f = n // tiles, n % tiles
        return rows(t, f * TOKENS, (f + 1) * TOKENS)

    total = jnp.zeros((TOKENS, WIDTH), jnp.float32)
    for n in range(count * tiles):
        x = block(n)
        total = total + x * x
    total = jnp.sum(total, axis=1, keepdims=True)
    rstd = lax.rsqrt(total * (1.0 / (count * tiles * WIDTH)) + EPSILON)
    last = tiles * TOKENS
    me = lax.axis_index("tp")
    for n in range(count * tiles):
        t, f = n // tiles, n % tiles
        column = pl.multiple_of(((me ^ t) * tiles + f) * WIDTH, WIDTH)
        gain = rows(t, last, last + 16)[f : f + 1]
        norm_ref[:, pl.ds(column, WIDTH)] = (block(n) * rstd * gain).astype(jnp.bfloat16)


def project_kernel(
    norm_ref, wq_ref, qg_ref, turn_ref, row_hbm,
    send_ref, pack_ref, norm_hbm, row_ref, sem,
):
    copies = [pltpu.make_async_copy(norm_ref, norm_hbm, sem.at[1])]
    copies[0].start()
    rows_copy = pltpu.make_async_copy(row_hbm, row_ref, sem.at[0])
    rows_copy.start()
    queries = jnp.dot(norm_ref[...], wq_ref[...], preferred_element_type=jnp.float32)
    cos, sin = unpacked(turn_ref[...])
    q_gain = qg_ref[...].astype(jnp.float32)
    low = lax.broadcasted_iota(jnp.int32, (8, WIDTH), 0) < STEPS
    turned = [
        rotated(queries[:, h * WIDTH : (h + 1) * WIDTH], q_gain, cos, sin)
        for h in range(HEADS)
    ]
    for i in range(ROWS // 2):
        parts = [turned[h][8 * i : 8 * i + 8] for h in range(HEADS)]
        rolled = [pltpu.roll(p, STEPS, 0) for p in parts]
        even = [jnp.where(low, parts[h], rolled[h + 1]) for h in (0, 2)]
        odd = [jnp.where(low, rolled[h], parts[h + 1]) for h in (0, 2)]
        pack_ref[2 * i] = jnp.concatenate(even, axis=0).astype(jnp.bfloat16)
        pack_ref[2 * i + 1] = jnp.concatenate(odd, axis=0).astype(jnp.bfloat16)
    me = lax.axis_index("dp")
    core = lax.rem(me, CORES)
    rows_copy.wait()
    for chip in range(CHIPS):
        for c in range(SHARED):
            holder = chip * CORES + (core if c < SLOTS else 1 - core)
            row = jnp.minimum(row_ref[holder, c % SLOTS, me], ROWS - 1)
            send_ref[chip, c * QUERIES : (c + 1) * QUERIES, :] = pack_ref[row]
    for copy in copies:
        copy.wait()


def fresh_kernel(
    norm_ref, wk_ref, wv_ref, kg_ref, turn_ref, pack_ref,
    key_ref, value_ref, max_ref, total_ref, out_ref,
):
    count = ROWS * QUERIES
    normed = norm_ref[...]
    keys = jnp.dot(normed, wk_ref[...], preferred_element_type=jnp.float32)
    keys = rotated(
        keys, kg_ref[...].astype(jnp.float32), *unpacked(turn_ref[...])
    ).astype(jnp.bfloat16)
    values = jnp.dot(normed, wv_ref[...], preferred_element_type=jnp.float32)
    values = values.astype(jnp.bfloat16)
    key_ref[...] = keys
    value_ref[...] = values
    scores = (
        lax.dot_general(
            pack_ref[...].reshape(count, WIDTH), keys,
            (((1,), (1,)), ((), ())), preferred_element_type=jnp.float32,
        )
        * SCALE
    )
    query = lax.broadcasted_iota(jnp.int32, (count, TOKENS), 0)
    token = lax.broadcasted_iota(jnp.int32, (count, TOKENS), 1)
    usable = ((query >> 4) == (token >> 2)) & ((token & 3) <= (query & 3))
    scores = jnp.where(usable, scores, MASKED)
    top = jnp.max(scores, axis=1, keepdims=True)
    weights = jnp.where(usable, jnp.exp(scores - top), 0.0).astype(jnp.bfloat16)
    total = jnp.sum(weights.astype(jnp.float32), axis=1, keepdims=True)
    out_ref[...] = jnp.dot(weights, values, preferred_element_type=jnp.float32)
    max_ref[...] = jnp.broadcast_to(top, (count, WIDTH))
    total_ref[...] = jnp.broadcast_to(total, (count, WIDTH))


def in_pieces(x):
    high = x.astype(jnp.bfloat16).astype(jnp.float32)
    rest = x - high
    middle = rest.astype(jnp.bfloat16).astype(jnp.float32)
    return [high, middle, rest - middle]


def page_kernel(
    q_ref, keep_ref, got_ref, cap_ref, send_ref, score_ref, weight_ref
):
    token = lax.broadcasted_iota(jnp.int32, (WIDTH, WIDTH), 0)
    member = lax.broadcasted_iota(jnp.int32, (WIDTH, WIDTH), 1) // QUERIES
    side_row = lax.broadcasted_iota(jnp.int32, (SIDE, WIDTH), 0)
    batches = GROUPS * SLOTS // 8
    pairs = SHARED * QUERIES

    def page(n, slot):
        chip, k, c = slot // SHARED, slot // SLOTS % CORES, slot % SLOTS
        return (keep_ref if k == 0 else got_ref)[n, chip, c]

    zero = jnp.zeros((), jnp.bfloat16)
    for j in range(batches):
        queries = q_ref[2 * j : 2 * j + 2].reshape(WIDTH, WIDTH)
        turned = queries.astype(jnp.float32).T.astype(jnp.bfloat16)
        keys = jnp.concatenate([page(0, 8 * j + i) for i in range(8)], axis=1)
        spread = jnp.concatenate([jnp.where(member == i, turned, zero) for i in range(8)], axis=0)
        scores = jnp.dot(keys, spread, preferred_element_type=jnp.float32) * SCALE
        score_ref[j * WIDTH : (j + 1) * WIDTH, :] = jnp.where(
            token < cap_ref[j : j + 1, :], scores, MASKED
        )
    for j in range(batches):
        scores = score_ref[j * WIDTH : (j + 1) * WIDTH, :]
        top = jnp.max(scores, axis=0, keepdims=True)
        weights = jnp.exp(scores - top).astype(jnp.bfloat16).astype(jnp.float32)
        total = jnp.sum(weights, axis=0, keepdims=True)
        weight_ref[j * WIDTH : (j + 1) * WIDTH, :] = weights.T.astype(jnp.bfloat16)
        tile = jnp.zeros((SIDE, WIDTH), jnp.float32)
        for n, piece in enumerate(in_pieces(top) + in_pieces(total)):
            tile = jnp.where(side_row == n, piece, tile)
        for k in range(2):
            send_ref[2 * j + k, pairs : pairs + SIDE, :] = tile.astype(jnp.bfloat16)
    for slot in range(0, GROUPS * SLOTS, 2):
        out = jnp.dot(
            weight_ref[slot * QUERIES : (slot + 2) * QUERIES, :],
            jnp.concatenate([page(1, slot), page(1, slot + 1)], axis=1),
            preferred_element_type=jnp.float32,
        )
        first = slot % SHARED * QUERIES
        out = jnp.concatenate([out[:QUERIES, :WIDTH], out[QUERIES:, WIDTH:]], axis=0)
        send_ref[slot // SHARED, first : first + 2 * QUERIES, :] = out.astype(jnp.bfloat16)


def combine_kernel(
    got_ref, max_ref, total_ref, out_ref, index_hbm,
    attention_hbm, attention_ref, top_wide, total_wide, index_ref, sem,
):
    index_copy = pltpu.make_async_copy(index_hbm, index_ref, sem.at[0])
    index_copy.start()
    me = lax.axis_index("dp")
    pairs = SHARED * QUERIES
    none = GROUPS * SLOTS
    sub = lax.broadcasted_iota(jnp.int32, (8, WIDTH), 0)
    tops, totals = [], []
    for b in range(CHIPS // 8):
        top_block = jnp.zeros((8, WIDTH), jnp.float32)
        total_block = jnp.zeros((8, WIDTH), jnp.float32)
        for i in range(8):
            tile = got_ref[8 * b + i, pairs : pairs + SIDE, :].astype(jnp.float32)
            top_block = jnp.where(sub == i, tile[0:1] + tile[1:2] + tile[2:3], top_block)
            total_block = jnp.where(sub == i, tile[3:4] + tile[4:5] + tile[5:6], total_block)
        tops.append(top_block)
        totals.append(total_block)
    side = jnp.concatenate(
        tops + totals + [jnp.zeros((WIDTH - 2 * CHIPS, WIDTH), jnp.float32)], axis=0
    )
    side = pltpu.roll(side, lax.rem((2 - lax.rem(me // CORES, 2)) * pairs, WIDTH), 1).T
    for chip in range(CHIPS):
        for c in range(SHARED):
            span = slice(c * QUERIES, (c + 1) * QUERIES)
            slot = chip * SHARED + c
            top_wide[slot] = jnp.broadcast_to(side[span, chip : chip + 1], (QUERIES, WIDTH))
            total_wide[slot] = jnp.broadcast_to(
                side[span, CHIPS + chip : CHIPS + chip + 1], (QUERIES, WIDTH)
            )
    top_wide[none] = jnp.full((QUERIES, WIDTH), MASKED, jnp.float32)
    total_wide[none] = jnp.zeros((QUERIES, WIDTH), jnp.float32)
    index_copy.wait()
    copies = []
    step = lax.broadcasted_iota(jnp.int32, (QUERIES, WIDTH), 0) & (STEPS - 1)
    for r in range(ROWS):
        span = slice(r * QUERIES, (r + 1) * QUERIES)
        tops, totals, outs = [max_ref[span, :]], [total_ref[span, :]], [out_ref[span, :]]
        for k in range(SLOTS):
            slot = index_ref[r * SLOTS + k]
            tops.append(top_wide[slot])
            totals.append(total_wide[slot])
            known = jnp.minimum(slot, none - 1)
            start = pl.multiple_of((known & (SHARED - 1)) * QUERIES, QUERIES)
            outs.append(got_ref[known >> 2, pl.ds(start, QUERIES), :].astype(jnp.float32))
        top = functools.reduce(jnp.maximum, tops)
        factors = [jnp.exp(t - top) for t in tops]
        above = sum(f * o for f, o in zip(factors, outs))
        below = sum(f * t for f, t in zip(factors, totals))
        result = jnp.where(step < index_ref[FIRST_LEFT + r], above / below, 0.0).astype(jnp.bfloat16)
        for h in range(HEADS):
            attention_ref[r, :, h * WIDTH : (h + 1) * WIDTH] = result[
                h * STEPS : (h + 1) * STEPS, :
            ]
        if r % 8 == 7:
            done = slice(r - 7, r + 1)
            copies.append(
                pltpu.make_async_copy(
                    attention_ref.at[done], attention_hbm.at[done], sem.at[1 + r // 8]
                )
            )
            copies[-1].start()
    for copy in copies:
        copy.wait()


SPREAD_MIB = 60
TABLE_MIB = 60
NORM_MIB = 4
NORM_COST = 20
PROJECT_MIB = 8
FRESH_MIB = 8
PAGES_MIB = 6
COMBINE_MIB = 6
TABLE_COST = 20
PROJECT_COST = 10
FRESH_COST = 10


def limit(mib):
    return pltpu.CompilerParams(vmem_limit_bytes=mib * 1024 * 1024)


def cost(us):
    return pl.CostEstimate(flops=us << 30, bytes_accessed=1 << 20, transcendentals=0)


def shards(
    hidden, norm_gain, w_query, key_projection, value_projection, query_gain, key_gain,
    cache_keys, cached_value_pages, cache_len, remaining, page_row, page_seq,
):
    features = hidden.shape[2]
    tensor = lax.axis_size("tp")
    bf16, f32 = jnp.bfloat16, jnp.float32
    width = tensor * features
    slots = GROUPS * SLOTS
    pairs = SHARED * QUERIES
    same_core = [[chip * CORES + core for chip in range(CHIPS)] for core in range(CORES)]
    flip = [(g, g ^ 1) for g in range(GROUPS)]
    vmem = pl.BlockSpec(memory_space=VMEM)
    smem = pl.BlockSpec(memory_space=SMEM)
    hbm = pl.BlockSpec(memory_space=pltpu.HBM)
    shape = jax.ShapeDtypeStruct
    dma = pltpu.SemaphoreType.DMA

    tiles = features // WIDTH
    rows = tiles * TOKENS + 16
    tiles = features // WIDTH
    rows = tiles * TOKENS + 16
    block = pl.pallas_call(
        block_kernel,
        out_shape=VMEM((rows, WIDTH), bf16),
        in_specs=[hbm, hbm],
        out_specs=vmem,
        scratch_shapes=[VMEM(hidden.shape, bf16), VMEM((tiles, WIDTH), bf16), dma((2,))],
        compiler_params=limit(SPREAD_MIB),
        name="block",
    )(hidden, norm_gain.reshape(tiles, WIDTH))

    def swapped(x, other):
        return lax.ppermute(x, "tp", [(t, t ^ other) for t in range(SHARDS)])

    def around(x):
        left, right = swapped(x, 2), swapped(x, 6)
        return left, swapped(left[:CUT], 6), swapped(right[CUT:], 2), right

    beside = swapped(block, 1)
    left, far_low, far_high, right = around(block)
    left_beside, low_beside, high_beside, right_beside = around(beside)
    gathered = (
        block, beside, left, left_beside, far_low, far_high, low_beside, high_beside,
        right, right_beside,
    )

    row_table = page_row.transpose(0, 2, 1)
    seq_table = page_seq.transpose(0, 2, 1)
    page_shape = (CHIPS, CORES, SLOTS, WIDTH, WIDTH)
    moved = (2, CHIPS, SLOTS, WIDTH, WIDTH)
    turns, caps, index, keep, give = pl.pallas_call(
        table_kernel,
        out_shape=(
            shape((TOKENS, WIDTH), f32), shape((slots // 8, WIDTH), jnp.int32),
            VMEM((INDEX,), jnp.int32),
            pltpu.HBM(moved, bf16), pltpu.HBM(moved, bf16),
        ),
        in_specs=[hbm] * 6,
        out_specs=(vmem,) * 3 + (hbm,) * 2,
        scratch_shapes=[
            VMEM((4, CHIPS, SLOTS, WIDTH, WIDTH), bf16), SMEM((INDEX,), jnp.int32),
            SMEM(cache_len.shape, jnp.int32), SMEM(remaining.shape, jnp.int32),
            SMEM(row_table.shape, jnp.int32), SMEM(seq_table.shape, jnp.int32), dma((13,)),
        ],
        compiler_params=limit(TABLE_MIB),
        cost_estimate=cost(TABLE_COST),
        name="tables",
    )(
        cache_keys.reshape(page_shape), cached_value_pages.reshape(page_shape),
        cache_len, remaining, row_table, seq_table,
    )
    got = lax.ppermute(give, "dp", flip)
    states = pl.pallas_call(
        norm_kernel,
        out_shape=VMEM((TOKENS, width), bf16),
        in_specs=[vmem] * len(gathered),
        out_specs=vmem,
        compiler_params=limit(NORM_MIB),
        cost_estimate=cost(NORM_COST),
        name="normalise",
    )(*gathered)
    send_q, pack, normed = pl.pallas_call(
        project_kernel,
        out_shape=(
            VMEM((CHIPS, pairs, WIDTH), bf16),
            shape((ROWS, QUERIES, WIDTH), bf16),
            pltpu.HBM((TOKENS, width), bf16),
        ),
        in_specs=[vmem] * 4 + [hbm],
        out_specs=(vmem, vmem, hbm),
        scratch_shapes=[SMEM(row_table.shape, jnp.int32), dma((2,))],
        compiler_params=limit(PROJECT_MIB),
        cost_estimate=cost(PROJECT_COST),
        name="project",
    )(states, w_query, query_gain[None, :], turns, row_table)
    got_q = lax.all_to_all(
        send_q, "dp", split_axis=0, concat_axis=0, tiled=True, axis_index_groups=same_core
    )
    new_key, new_value, new_max, new_total, new_out = pl.pallas_call(
        fresh_kernel,
        out_shape=(shape((TOKENS, WIDTH), bf16),) * 2
        + (shape((ROWS * QUERIES, WIDTH), f32),) * 3,
        in_specs=[vmem] * 6,
        out_specs=(vmem,) * 5,
        compiler_params=limit(FRESH_MIB),
        cost_estimate=cost(FRESH_COST),
        name="fresh",
    )(normed, key_projection, value_projection, key_gain[None, :], turns, pack)
    send_out = pl.pallas_call(
        page_kernel,
        out_shape=VMEM((CHIPS, pairs + SIDE, WIDTH), bf16),
        in_specs=[vmem] * 4,
        out_specs=vmem,
        scratch_shapes=[
            VMEM((slots * QUERIES, WIDTH), f32),
            VMEM((slots * QUERIES, WIDTH), bf16),
        ],
        compiler_params=limit(PAGES_MIB),
        name="pages",
    )(
        got_q, keep, got, caps,
    )
    got_out = lax.all_to_all(
        send_out, "dp", split_axis=0, concat_axis=0, tiled=True, axis_index_groups=same_core
    )
    attention = pl.pallas_call(
        combine_kernel,
        out_shape=pltpu.HBM((ROWS, STEPS, HEADS * WIDTH), bf16),
        in_specs=[vmem] * 4 + [hbm],
        out_specs=hbm,
        scratch_shapes=[
            VMEM((ROWS, STEPS, HEADS * WIDTH), bf16),
            VMEM((slots + 1, QUERIES, WIDTH), f32),
            VMEM((slots + 1, QUERIES, WIDTH), f32),
            SMEM((INDEX,), jnp.int32),
            dma((1 + ROWS // 8,)),
        ],
        compiler_params=limit(COMBINE_MIB),
        name="combine",
    )(got_out, new_max, new_total, new_out, index)
    return (
        attention,
        new_key.reshape(ROWS, STEPS, WIDTH),
        new_value.reshape(ROWS, STEPS, WIDTH),
    )


def solution(mesh):
    in_specs = (
        P("dp", None, "tp"),
        P("tp"),
        P(None, "tp"),
        P(None, "tp"),
        P(None, "tp"),
        P(),
        P(),
        P("dp", None, None, None, "tp"),
        P("dp", None, None, None, "tp"),
        P(),
        P("dp"),
        P(),
        P(),
    )
    out_specs = (P("dp", None, "tp"), P("dp", None, "tp"), P("dp", None, "tp"))
    return jax.shard_map(shards, mesh=mesh, in_specs=in_specs, out_specs=out_specs, check_vma=False)
```

```python
import functools
import math

import jax
import jax.numpy as jnp
from jax import lax
from jax.experimental import pallas as pl
from jax.experimental.pallas import tpu as pltpu
from jax.sharding import PartitionSpec as P

EPSILON = 1e-06
ROPE_BASE = 1000000.0
MASKED = -1e30
ROWS = 32
STEPS = 4
HEADS = 4
QUERIES = HEADS * STEPS
WIDTH = 128
GROUPS = 32
CORES = 2
CHIPS = GROUPS // CORES
SLOTS = 2
FIRST_LEFT = 96
FIRST_ROW = 128
INDEX = 1024
SHARDS = 8
CUT = 320
SHARED = CORES * SLOTS
TOKENS = ROWS * STEPS
SIDE = 8
SCALE = 1.0 / math.sqrt(WIDTH)

VMEM = pltpu.VMEM
SMEM = pltpu.SMEM


def block_kernel(hidden_hbm, gain_hbm, block_ref, hidden_ref, gain_ref, sem):
    copies = [
        pltpu.make_async_copy(hidden_hbm, hidden_ref, sem.at[0]),
        pltpu.make_async_copy(gain_hbm, gain_ref, sem.at[1]),
    ]
    for copy in copies:
        copy.start()
    for copy in copies:
        copy.wait()
    tiles = hidden_hbm.shape[2] // WIDTH
    for i in range(0, ROWS, 4):
        part = [hidden_ref[i + k].astype(jnp.float32) for k in range(4)]
        part = jnp.concatenate(part, axis=0).astype(jnp.bfloat16)
        for f in range(tiles):
            first = f * TOKENS + i * STEPS
            block_ref[first : first + 4 * STEPS, :] = part[:, f * WIDTH : (f + 1) * WIDTH]
    gain = gain_ref[...].astype(jnp.float32)
    gain = jnp.concatenate([gain, jnp.zeros((16 - tiles, WIDTH), jnp.float32)], axis=0)
    block_ref[tiles * TOKENS : tiles * TOKENS + 16, :] = gain.astype(jnp.bfloat16)


def table_kernel(
    key_hbm, value_hbm, len_hbm, left_hbm, row_hbm, seq_hbm,
    turn_out, cap_out, index_out, keep_hbm, give_hbm,
    stage_ref, index_ref, len_ref, left_ref, row_ref, seq_ref, sem,
):
    scalars = [
        pltpu.make_async_copy(source, target, sem.at[9 + n])
        for n, (source, target) in enumerate(
            ((len_hbm, len_ref), (left_hbm, left_ref), (row_hbm, row_ref), (seq_hbm, seq_ref))
        )
    ]
    for copy in scalars:
        copy.start()
    me = lax.axis_index("dp")
    core = lax.rem(me, CORES)
    arrivals, departures = [], []
    for target, half in ((give_hbm, 1 - core), (keep_hbm, core)):
        for n, pages in enumerate((key_hbm, value_hbm)):
            place = len(arrivals)
            staged = stage_ref.at[place]
            arrivals.append(pltpu.make_async_copy(pages.at[:, half], staged, sem.at[place]))
            departures.append(pltpu.make_async_copy(staged, target.at[n], sem.at[4 + place]))
    for copy in arrivals:
        copy.start()
    for arrival, departure in zip(arrivals, departures):
        arrival.wait()
        departure.start()
    for copy in scalars:
        copy.wait()
    half = TOKENS // 2
    token = lax.broadcasted_iota(jnp.int32, (half, WIDTH), 0)
    column = lax.broadcasted_iota(jnp.int32, (half, WIDTH), 1)
    left = column < WIDTH // 2
    position = token & (STEPS - 1)
    for r in range(ROWS // 2):
        length = jnp.where(left, len_ref[me * ROWS + r], len_ref[me * ROWS + ROWS // 2 + r])
        position = position + jnp.where(token // STEPS == r, length, 0)
    pair = (column & (WIDTH // 2 - 1)).astype(jnp.float32)
    angle = position.astype(jnp.float32) * jnp.exp(pair * (-2.0 * math.log(ROPE_BASE) / WIDTH))
    cos, sin = jnp.cos(angle), jnp.sin(angle)
    turn_out[:half, :] = jnp.where(left, cos, pltpu.roll(sin, WIDTH // 2, 1))
    turn_out[half:, :] = jnp.where(left, pltpu.roll(cos, WIDTH // 2, 1), sin)
    lane = lax.broadcasted_iota(jnp.int32, (1, WIDTH), 1) // QUERIES
    for j in range(GROUPS * SLOTS // 8):
        cap = jnp.zeros((1, WIDTH), jnp.int32)
        for i in range(8):
            chip, k, c = 2 * j + i // SHARED, i // SLOTS % CORES, i % SLOTS
            owner = chip * CORES + core
            holder = me if k == 0 else me + 1 - 2 * core
            row = row_ref[holder, c, owner]
            length = len_ref[owner * ROWS + jnp.minimum(row, ROWS - 1)]
            cap = jnp.where(
                lane == i, jnp.where(row < ROWS, length - seq_ref[holder, c, owner] * WIDTH, 0), cap
            )
        cap_out[j : j + 1, :] = cap
    none = GROUPS * SLOTS
    for i in range(none + 1):
        index_ref[i] = none
    for chip in range(CHIPS):
        for c in range(SHARED):
            holder = chip * CORES + (core if c < SLOTS else 1 - core)
            row = row_ref[holder, c % SLOTS, me]
            seq = seq_ref[holder, c % SLOTS, me]
            slot = chip * SHARED + c
            index_ref[jnp.where(row < ROWS, row * SLOTS + seq, none)] = slot
            index_ref[FIRST_ROW + slot] = jnp.minimum(row, ROWS - 1)
    for r in range(ROWS):
        index_ref[FIRST_LEFT + r] = left_ref[r]
    index_copy = pltpu.make_async_copy(index_ref, index_out, sem.at[8])
    index_copy.start()
    for departure in departures:
        departure.wait()
    index_copy.wait()


def unpacked(turn):
    other = pltpu.roll(turn, WIDTH // 2, 1)
    left = lax.broadcasted_iota(jnp.int32, turn.shape, 1) < WIDTH // 2
    return jnp.where(left, turn, other), jnp.where(left, -other, turn)


def rotated(heads, gain, cos, sin):
    mean = jnp.sum(heads * heads, axis=1, keepdims=True) * (1.0 / WIDTH)
    scaled = heads * lax.rsqrt(mean + EPSILON) * gain
    return scaled * cos + pltpu.roll(scaled, WIDTH // 2, 1) * sin


def norm_kernel(*refs):
    shards, norm_ref = refs[:-1], refs[-1]
    count = SHARDS
    tiles = norm_ref.shape[1] // count // WIDTH
    pieces = {0: (0,), 1: (1,), 2: (2,), 3: (3,), 4: (4, 5), 5: (6, 7), 6: (8,), 7: (9,)}

    def rows(t, first, last):
        held = pieces[t]
        if len(held) == 1:
            return shards[held[0]][first:last, :].astype(jnp.float32)
        if last <= CUT:
            return shards[held[0]][first:last, :].astype(jnp.float32)
        if first >= CUT:
            return shards[held[1]][first - CUT : last - CUT, :].astype(jnp.float32)
        return jnp.concatenate([rows(t, first, CUT), rows(t, CUT, last)], axis=0)

    def block(n):
        t, f = n // tiles, n % tiles
        return rows(t, f * TOKENS, (f + 1) * TOKENS)

    total = jnp.zeros((TOKENS, WIDTH), jnp.float32)
    for n in range(count * tiles):
        x = block(n)
        total = total + x * x
    total = jnp.sum(total, axis=1, keepdims=True)
    rstd = lax.rsqrt(total * (1.0 / (count * tiles * WIDTH)) + EPSILON)
    last = tiles * TOKENS
    me = lax.axis_index("tp")
    for n in range(count * tiles):
        t, f = n // tiles, n % tiles
        column = pl.multiple_of(((me ^ t) * tiles + f) * WIDTH, WIDTH)
        gain = rows(t, last, last + 16)[f : f + 1]
        norm_ref[:, pl.ds(column, WIDTH)] = (block(n) * rstd * gain).astype(jnp.bfloat16)


def project_kernel(
    norm_ref, wq_ref, qg_ref, turn_ref, row_hbm,
    send_ref, pack_ref, norm_hbm, row_ref, sem,
):
    copies = [pltpu.make_async_copy(norm_ref, norm_hbm, sem.at[1])]
    copies[0].start()
    rows_copy = pltpu.make_async_copy(row_hbm, row_ref, sem.at[0])
    rows_copy.start()
    queries = jnp.dot(norm_ref[...], wq_ref[...], preferred_element_type=jnp.float32)
    cos, sin = unpacked(turn_ref[...])
    q_gain = qg_ref[...].astype(jnp.float32)
    low = lax.broadcasted_iota(jnp.int32, (8, WIDTH), 0) < STEPS
    turned = [
        rotated(queries[:, h * WIDTH : (h + 1) * WIDTH], q_gain, cos, sin)
        for h in range(HEADS)
    ]
    for i in range(ROWS // 2):
        parts = [turned[h][8 * i : 8 * i + 8] for h in range(HEADS)]
        rolled = [pltpu.roll(p, STEPS, 0) for p in parts]
        even = [jnp.where(low, parts[h], rolled[h + 1]) for h in (0, 2)]
        odd = [jnp.where(low, rolled[h], parts[h + 1]) for h in (0, 2)]
        pack_ref[2 * i] = jnp.concatenate(even, axis=0).astype(jnp.bfloat16)
        pack_ref[2 * i + 1] = jnp.concatenate(odd, axis=0).astype(jnp.bfloat16)
    me = lax.axis_index("dp")
    core = lax.rem(me, CORES)
    rows_copy.wait()
    for chip in range(CHIPS):
        for c in range(SHARED):
            holder = chip * CORES + (core if c < SLOTS else 1 - core)
            row = jnp.minimum(row_ref[holder, c % SLOTS, me], ROWS - 1)
            send_ref[chip, c * QUERIES : (c + 1) * QUERIES, :] = pack_ref[row]
    for copy in copies:
        copy.wait()


def fresh_kernel(
    norm_ref, wk_ref, wv_ref, kg_ref, turn_ref, pack_ref,
    key_ref, value_ref, max_ref, total_ref, out_ref,
):
    count = ROWS * QUERIES
    normed = norm_ref[...]
    keys = jnp.dot(normed, wk_ref[...], preferred_element_type=jnp.float32)
    keys = rotated(
        keys, kg_ref[...].astype(jnp.float32), *unpacked(turn_ref[...])
    ).astype(jnp.bfloat16)
    values = jnp.dot(normed, wv_ref[...], preferred_element_type=jnp.float32)
    values = values.astype(jnp.bfloat16)
    key_ref[...] = keys
    value_ref[...] = values
    scores = (
        lax.dot_general(
            pack_ref[...].reshape(count, WIDTH), keys,
            (((1,), (1,)), ((), ())), preferred_element_type=jnp.float32,
        )
        * SCALE
    )
    query = lax.broadcasted_iota(jnp.int32, (count, TOKENS), 0)
    token = lax.broadcasted_iota(jnp.int32, (count, TOKENS), 1)
    usable = ((query >> 4) == (token >> 2)) & ((token & 3) <= (query & 3))
    scores = jnp.where(usable, scores, MASKED)
    top = jnp.max(scores, axis=1, keepdims=True)
    weights = jnp.where(usable, jnp.exp(scores - top), 0.0).astype(jnp.bfloat16)
    total = jnp.sum(weights.astype(jnp.float32), axis=1, keepdims=True)
    out_ref[...] = jnp.dot(weights, values, preferred_element_type=jnp.float32)
    max_ref[...] = jnp.broadcast_to(top, (count, WIDTH))
    total_ref[...] = jnp.broadcast_to(total, (count, WIDTH))


def in_pieces(x):
    high = x.astype(jnp.bfloat16).astype(jnp.float32)
    rest = x - high
    middle = rest.astype(jnp.bfloat16).astype(jnp.float32)
    return [high, middle, rest - middle]


def page_kernel(
    q_ref, keep_ref, got_ref, cap_ref, send_ref, score_ref, weight_ref
):
    token = lax.broadcasted_iota(jnp.int32, (WIDTH, WIDTH), 0)
    member = lax.broadcasted_iota(jnp.int32, (WIDTH, WIDTH), 1) // QUERIES
    side_row = lax.broadcasted_iota(jnp.int32, (SIDE, WIDTH), 0)
    batches = GROUPS * SLOTS // 8
    pairs = SHARED * QUERIES

    def page(n, slot):
        chip, k, c = slot // SHARED, slot // SLOTS % CORES, slot % SLOTS
        return (keep_ref if k == 0 else got_ref)[n, chip, c]

    zero = jnp.zeros((), jnp.bfloat16)
    for j in range(batches):
        queries = q_ref[2 * j : 2 * j + 2].reshape(WIDTH, WIDTH)
        turned = queries.astype(jnp.float32).T.astype(jnp.bfloat16)
        keys = jnp.concatenate([page(0, 8 * j + i) for i in range(8)], axis=1)
        spread = jnp.concatenate([jnp.where(member == i, turned, zero) for i in range(8)], axis=0)
        scores = jnp.dot(keys, spread, preferred_element_type=jnp.float32) * SCALE
        score_ref[j * WIDTH : (j + 1) * WIDTH, :] = jnp.where(
            token < cap_ref[j : j + 1, :], scores, MASKED
        )
    for j in range(batches):
        scores = score_ref[j * WIDTH : (j + 1) * WIDTH, :]
        top = jnp.max(scores, axis=0, keepdims=True)
        weights = jnp.exp(scores - top).astype(jnp.bfloat16).astype(jnp.float32)
        total = jnp.sum(weights, axis=0, keepdims=True)
        weight_ref[j * WIDTH : (j + 1) * WIDTH, :] = weights.T.astype(jnp.bfloat16)
        tile = jnp.zeros((SIDE, WIDTH), jnp.float32)
        for n, piece in enumerate(in_pieces(top) + in_pieces(total)):
            tile = jnp.where(side_row == n, piece, tile)
        for k in range(2):
            send_ref[2 * j + k, pairs : pairs + SIDE, :] = tile.astype(jnp.bfloat16)
    for slot in range(0, GROUPS * SLOTS, 2):
        out = jnp.dot(
            weight_ref[slot * QUERIES : (slot + 2) * QUERIES, :],
            jnp.concatenate([page(1, slot), page(1, slot + 1)], axis=1),
            preferred_element_type=jnp.float32,
        )
        first = slot % SHARED * QUERIES
        out = jnp.concatenate([out[:QUERIES, :WIDTH], out[QUERIES:, WIDTH:]], axis=0)
        send_ref[slot // SHARED, first : first + 2 * QUERIES, :] = out.astype(jnp.bfloat16)


def combine_kernel(
    got_ref, max_ref, total_ref, out_ref, index_hbm,
    attention_hbm, attention_ref, top_wide, total_wide, index_ref, sem,
):
    index_copy = pltpu.make_async_copy(index_hbm, index_ref, sem.at[0])
    index_copy.start()
    me = lax.axis_index("dp")
    pairs = SHARED * QUERIES
    none = GROUPS * SLOTS
    sub = lax.broadcasted_iota(jnp.int32, (8, WIDTH), 0)
    tops, totals = [], []
    for b in range(CHIPS // 8):
        top_block = jnp.zeros((8, WIDTH), jnp.float32)
        total_block = jnp.zeros((8, WIDTH), jnp.float32)
        for i in range(8):
            tile = got_ref[8 * b + i, pairs : pairs + SIDE, :].astype(jnp.float32)
            top_block = jnp.where(sub == i, tile[0:1] + tile[1:2] + tile[2:3], top_block)
            total_block = jnp.where(sub == i, tile[3:4] + tile[4:5] + tile[5:6], total_block)
        tops.append(top_block)
        totals.append(total_block)
    side = jnp.concatenate(
        tops + totals + [jnp.zeros((WIDTH - 2 * CHIPS, WIDTH), jnp.float32)], axis=0
    )
    side = pltpu.roll(side, lax.rem((2 - lax.rem(me // CORES, 2)) * pairs, WIDTH), 1).T
    for chip in range(CHIPS):
        for c in range(SHARED):
            span = slice(c * QUERIES, (c + 1) * QUERIES)
            slot = chip * SHARED + c
            top_wide[slot] = jnp.broadcast_to(side[span, chip : chip + 1], (QUERIES, WIDTH))
            total_wide[slot] = jnp.broadcast_to(
                side[span, CHIPS + chip : CHIPS + chip + 1], (QUERIES, WIDTH)
            )
    top_wide[none] = jnp.full((QUERIES, WIDTH), MASKED, jnp.float32)
    total_wide[none] = jnp.zeros((QUERIES, WIDTH), jnp.float32)
    index_copy.wait()
    copies = []
    step = lax.broadcasted_iota(jnp.int32, (QUERIES, WIDTH), 0) & (STEPS - 1)
    for r in range(ROWS):
        span = slice(r * QUERIES, (r + 1) * QUERIES)
        tops, totals, outs = [max_ref[span, :]], [total_ref[span, :]], [out_ref[span, :]]
        for k in range(SLOTS):
            slot = index_ref[r * SLOTS + k]
            tops.append(top_wide[slot])
            totals.append(total_wide[slot])
            known = jnp.minimum(slot, none - 1)
            start = pl.multiple_of((known & (SHARED - 1)) * QUERIES, QUERIES)
            outs.append(got_ref[known >> 2, pl.ds(start, QUERIES), :].astype(jnp.float32))
        top = functools.reduce(jnp.maximum, tops)
        factors = [jnp.exp(t - top) for t in tops]
        above = sum(f * o for f, o in zip(factors, outs))
        below = sum(f * t for f, t in zip(factors, totals))
        result = jnp.where(step < index_ref[FIRST_LEFT + r], above / below, 0.0).astype(jnp.bfloat16)
        for h in range(HEADS):
            attention_ref[r, :, h * WIDTH : (h + 1) * WIDTH] = result[
                h * STEPS : (h + 1) * STEPS, :
            ]
        if r % 8 == 7:
            done = slice(r - 7, r + 1)
            copies.append(
                pltpu.make_async_copy(
                    attention_ref.at[done], attention_hbm.at[done], sem.at[1 + r // 8]
                )
            )
            copies[-1].start()
    for copy in copies:
        copy.wait()


SPREAD_MIB = 60
TABLE_MIB = 60
NORM_MIB = 4
NORM_COST = 20
PROJECT_MIB = 8
FRESH_MIB = 8
PAGES_MIB = 6
COMBINE_MIB = 6
TABLE_COST = 20
PROJECT_COST = 10
FRESH_COST = 10


def limit(mib):
    return pltpu.CompilerParams(vmem_limit_bytes=mib * 1024 * 1024)


def cost(us):
    return pl.CostEstimate(flops=us << 30, bytes_accessed=1 << 20, transcendentals=0)


def shards(
    hidden, norm_gain, w_query, key_projection, value_projection, query_gain, key_gain,
    cache_keys, cached_value_pages, cache_len, remaining, page_row, page_seq,
):
    features = hidden.shape[2]
    tensor = lax.axis_size("tp")
    bf16, f32 = jnp.bfloat16, jnp.float32
    width = tensor * features
    slots = GROUPS * SLOTS
    pairs = SHARED * QUERIES
    same_core = [[chip * CORES + core for chip in range(CHIPS)] for core in range(CORES)]
    flip = [(g, g ^ 1) for g in range(GROUPS)]
    vmem = pl.BlockSpec(memory_space=VMEM)
    smem = pl.BlockSpec(memory_space=SMEM)
    hbm = pl.BlockSpec(memory_space=pltpu.HBM)
    shape = jax.ShapeDtypeStruct
    dma = pltpu.SemaphoreType.DMA

    tiles = features // WIDTH
    rows = tiles * TOKENS + 16
    tiles = features // WIDTH
    rows = tiles * TOKENS + 16
    block = pl.pallas_call(
        block_kernel,
        out_shape=VMEM((rows, WIDTH), bf16),
        in_specs=[hbm, hbm],
        out_specs=vmem,
        scratch_shapes=[VMEM(hidden.shape, bf16), VMEM((tiles, WIDTH), bf16), dma((2,))],
        compiler_params=limit(SPREAD_MIB),
        name="block",
    )(hidden, norm_gain.reshape(tiles, WIDTH))

    def swapped(x, other):
        return lax.ppermute(x, "tp", [(t, t ^ other) for t in range(SHARDS)])

    def around(x):
        left, right = swapped(x, 2), swapped(x, 6)
        return left, swapped(left[:CUT], 6), swapped(right[CUT:], 2), right

    beside = swapped(block, 1)
    left, far_low, far_high, right = around(block)
    left_beside, low_beside, high_beside, right_beside = around(beside)
    gathered = (
        block, beside, left, left_beside, far_low, far_high, low_beside, high_beside,
        right, right_beside,
    )

    row_table = page_row.transpose(0, 2, 1)
    seq_table = page_seq.transpose(0, 2, 1)
    page_shape = (CHIPS, CORES, SLOTS, WIDTH, WIDTH)
    moved = (2, CHIPS, SLOTS, WIDTH, WIDTH)
    turns, caps, index, keep, give = pl.pallas_call(
        table_kernel,
        out_shape=(
            shape((TOKENS, WIDTH), f32), shape((slots // 8, WIDTH), jnp.int32),
            VMEM((INDEX,), jnp.int32),
            pltpu.HBM(moved, bf16), pltpu.HBM(moved, bf16),
        ),
        in_specs=[hbm] * 6,
        out_specs=(vmem,) * 3 + (hbm,) * 2,
        scratch_shapes=[
            VMEM((4, CHIPS, SLOTS, WIDTH, WIDTH), bf16), SMEM((INDEX,), jnp.int32),
            SMEM(cache_len.shape, jnp.int32), SMEM(remaining.shape, jnp.int32),
            SMEM(row_table.shape, jnp.int32), SMEM(seq_table.shape, jnp.int32), dma((13,)),
        ],
        compiler_params=limit(TABLE_MIB),
        cost_estimate=cost(TABLE_COST),
        name="tables",
    )(
        cache_keys.reshape(page_shape), cached_value_pages.reshape(page_shape),
        cache_len, remaining, row_table, seq_table,
    )
    got = lax.ppermute(give, "dp", flip)
    states = pl.pallas_call(
        norm_kernel,
        out_shape=VMEM((TOKENS, width), bf16),
        in_specs=[vmem] * len(gathered),
        out_specs=vmem,
        compiler_params=limit(NORM_MIB),
        cost_estimate=cost(NORM_COST),
        name="normalise",
    )(*gathered)
    send_q, pack, normed = pl.pallas_call(
        project_kernel,
        out_shape=(
            VMEM((CHIPS, pairs, WIDTH), bf16),
            shape((ROWS, QUERIES, WIDTH), bf16),
            pltpu.HBM((TOKENS, width), bf16),
        ),
        in_specs=[vmem] * 4 + [hbm],
        out_specs=(vmem, vmem, hbm),
        scratch_shapes=[SMEM(row_table.shape, jnp.int32), dma((2,))],
        compiler_params=limit(PROJECT_MIB),
        cost_estimate=cost(PROJECT_COST),
        name="project",
    )(states, w_query, query_gain[None, :], turns, row_table)
    got_q = lax.all_to_all(
        send_q, "dp", split_axis=0, concat_axis=0, tiled=True, axis_index_groups=same_core
    )
    new_key, new_value, new_max, new_total, new_out = pl.pallas_call(
        fresh_kernel,
        out_shape=(shape((TOKENS, WIDTH), bf16),) * 2
        + (shape((ROWS * QUERIES, WIDTH), f32),) * 3,
        in_specs=[vmem] * 6,
        out_specs=(vmem,) * 5,
        compiler_params=limit(FRESH_MIB),
        cost_estimate=cost(FRESH_COST),
        name="fresh",
    )(normed, key_projection, value_projection, key_gain[None, :], turns, pack)
    send_out = pl.pallas_call(
        page_kernel,
        out_shape=VMEM((CHIPS, pairs + SIDE, WIDTH), bf16),
        in_specs=[vmem] * 4,
        out_specs=vmem,
        scratch_shapes=[
            VMEM((slots * QUERIES, WIDTH), f32),
            VMEM((slots * QUERIES, WIDTH), bf16),
        ],
        compiler_params=limit(PAGES_MIB),
        name="pages",
    )(
        got_q, keep, got, caps,
    )
    got_out = lax.all_to_all(
        send_out, "dp", split_axis=0, concat_axis=0, tiled=True, axis_index_groups=same_core
    )
    attention = pl.pallas_call(
        combine_kernel,
        out_shape=pltpu.HBM((ROWS, STEPS, HEADS * WIDTH), bf16),
        in_specs=[vmem] * 4 + [hbm],
        out_specs=hbm,
        scratch_shapes=[
            VMEM((ROWS, STEPS, HEADS * WIDTH), bf16),
            VMEM((slots + 1, QUERIES, WIDTH), f32),
            VMEM((slots + 1, QUERIES, WIDTH), f32),
            SMEM((INDEX,), jnp.int32),
            dma((1 + ROWS // 8,)),
        ],
        compiler_params=limit(COMBINE_MIB),
        name="combine",
    )(got_out, new_max, new_total, new_out, index)
    return (
        attention,
        new_key.reshape(ROWS, STEPS, WIDTH),
        new_value.reshape(ROWS, STEPS, WIDTH),
    )


def solution(mesh):
    in_specs = (
        P("dp", None, "tp"),
        P("tp"),
        P(None, "tp"),
        P(None, "tp"),
        P(None, "tp"),
        P(),
        P(),
        P("dp", None, None, None, "tp"),
        P("dp", None, None, None, "tp"),
        P(),
        P("dp"),
        P(),
        P(),
    )
    out_specs = (P("dp", None, "tp"), P("dp", None, "tp"), P("dp", None, "tp"))
    return jax.shard_map(shards, mesh=mesh, in_specs=in_specs, out_specs=out_specs, check_vma=False)
```
